32 devices in a mesh: grp: 2 (over y), seq: 16 (over z, x, core).
Axes of the slice: x: 2, y: 2, z: 4, core: 2. Of those that a mesh axis runs over, the one named last changes fastest.
Arguments:
- gate_out: bfloat16 [8192, 4096], P(('grp', 'seq')), parts along dimension 0, may hold values from -6 to 6
- gate_in: bfloat16 [8192, 4096], P(('grp', 'seq')), parts along dimension 0, may hold values from -6 to 6
- values: bfloat16 [8192, 4096], P(('grp', 'seq')), parts along dimension 0, may hold values from -6 to 6
- gate_mid: bfloat16 [8192, 4096], P(('grp', 'seq')), parts along dimension 0, may hold values from -6 to 6
- medium_taps: bfloat16 [256, 128], replicated, may hold values from -0.5 to 0.5
- medium_skip: float32 [4096], replicated, may hold values from -3 to 3
- residues: float32 [256, 16], replicated, may hold values from -1 to 1, as said below
- rates: float32 [256, 16], replicated, may hold values from 0 to 0.1, as said below
- long_skip: float32 [4096], replicated, may hold values from -3 to 3
Outputs:
- mixed: bfloat16 [8192, 4096], P(('grp', 'seq')), parts along dimension 0
The draws below stay inside these ranges and needn't reach their ends.
There are 2 independent parts, one for each index of `grp`. The reference program is written for one: setup_inputs(seed, part) draws one part's arguments, and reference() takes and returns one part's arrays. A program takes and returns all parts, laid end to end along the dimension named above; an argument that names none is the same for every part. Nothing has to cross between parts.
Inputs may be any that keep to these rules, and one draw needn't show every extreme that they name: Positive rates; each pole's filter falls by exp(-rate) per position. Real residues of the poles.
All inputs are finite; a program needn't handle non-finite values.
Results may differ from the reference program's by a relative error of at most 0.0061.
Values may be sent and summed in bfloat16 or wider, within the bound.
A program may use at most 192 MiB of HBM per device.

```python
import jax
import jax.numpy as jnp
from jax import lax

D = 4096
GROUP = 16
GROUPS = 256
MED = 128
POLES = 16
SUB = 128
TOK_DEV = 256
LENGTH = 4096
N_SEQ = 16


def pole_table(key):
    base = jax.random.fold_in(key, 17)
    pick_key, slow_key, fast_key = jax.random.split(base, 3)
    groups = D // GROUP
    slow_share = 0.5
    slow_mask = jax.random.uniform(pick_key, (groups, POLES)) < slow_share
    slow_rate = jnp.exp(jax.random.uniform(slow_key, (groups, POLES), minval=jnp.log(0.05 / LENGTH), maxval=jnp.log(2.3 / LENGTH)))
    fast_rate = jnp.exp(jax.random.uniform(fast_key, (groups, POLES), minval=jnp.log(0.02), maxval=jnp.log(0.1)))
    return jnp.where(slow_mask, slow_rate, fast_rate).astype(jnp.float32)


def draw_rates(key, part):
    return pole_table(key)


def draw_residues(key, part):
    rate_values = pole_table(key)
    noise_key = jax.random.fold_in(key, 29)
    noise_values = jnp.clip(jax.random.normal(noise_key, rate_values.shape), -6.0, 6.0)
    return (noise_values * jnp.sqrt(2.0 * rate_values / POLES)).astype(jnp.float32)


def levels(own_key, extent, cuts, least, high):
    factor_of, own = 1.0, jax.random.fold_in(own_key, 6)
    for position, shards_of in cuts:
        draws = jnp.exp(jax.random.uniform(jax.random.fold_in(own, position), (shards_of,), jnp.float32, least / len(cuts), high / len(cuts)))
        factor_of = factor_of * jnp.repeat(draws, extent[position] // shards_of).reshape([-1 if axis == position else 1 for axis in range(len(extent))])
    return factor_of


def bell_draw(own_key, dims, width, bound, cuts=(), kind=jnp.bfloat16):
    drawn = jax.random.normal(own_key, dims, jnp.float32) * width
    if len(cuts) > 0:
        drawn = levels(own_key, dims, cuts, -0.22, 0.18) * drawn
    return jnp.clip(drawn, min=-bound, max=bound).astype(kind)


def setup_inputs(seed: int = 0, part: int = 0) -> dict:
    splits = jax.random.split(jax.random.key(seed), 10)
    part_splits = jax.random.split(jax.random.fold_in(splits[9], part), 10)
    return {
        "gate_out": bell_draw(part_splits[0], (LENGTH, D), 1.0, 6.0, ((0, 16),)),
        "gate_in": bell_draw(part_splits[1], (LENGTH, D), 1.0, 6.0, ((0, 16),)),
        "values": bell_draw(part_splits[2], (LENGTH, D), 1.0, 6.0, ((0, 16),)),
        "gate_mid": bell_draw(part_splits[3], (LENGTH, D), 1.0, 6.0, ((0, 16),)),
        "medium_taps": bell_draw(splits[4], (GROUPS, MED), MED ** -0.5, 0.5),
        "medium_skip": bell_draw(splits[5], (D,), 0.5, 3.0, (), jnp.float32),
        "residues": draw_residues(jax.random.fold_in(splits[9], 71), part),
        "rates": draw_rates(jax.random.fold_in(splits[9], 71), part),
        "long_skip": bell_draw(splits[8], (D,), 0.5, 3.0, (), jnp.float32),
    }


def banded(tap_values, out_rows, in_cols):
    group_count, tap_count = tap_values.shape
    line = jnp.concatenate([jnp.zeros((group_count, in_cols - tap_count), tap_values.dtype), tap_values[:, ::-1], jnp.zeros((group_count, out_rows - 1), tap_values.dtype)], axis=1)
    cycle = jnp.concatenate([line[:, out_rows - 1:], jnp.zeros((group_count, 1), tap_values.dtype), line[:, :out_rows - 1]], axis=1)
    period = cycle.shape[1]
    tiled = jnp.tile(cycle, (1, out_rows))[:, :out_rows * (period - 1)]
    return tiled.reshape(group_count, out_rows, period - 1)[:, :, :in_cols]


def reference(gate_out, gate_in, values, gate_mid, medium_taps, medium_skip, residues, rates, long_skip):
    block_count = TOK_DEV // SUB
    maximum_level = lax.Precision.HIGHEST
    middle_filter_matrix = banded(medium_taps, SUB, 2 * SUB).astype(jnp.float32)
    offsets = jnp.arange(SUB).astype(jnp.float32)
    decay_up = jnp.exp(-rates[:, :, None] * offsets)
    long_taps = jnp.einsum("gp,gpn->gn", residues, decay_up, precision=maximum_level).astype(jnp.bfloat16)
    short_filter_matrix = banded(long_taps, SUB, SUB).astype(jnp.float32)
    fold_weights = jnp.exp(-rates[:, :, None] * (SUB - 1.0 - offsets)).astype(jnp.bfloat16).astype(jnp.float32)
    distance_weight = residues[:, :, None] * jnp.exp(-rates[:, :, None] * (offsets + 1.0))
    step_decay = jnp.exp(-rates * SUB)[:, :, None]

    def sub_step(held_state, sub_state):
        return step_decay * held_state + sub_state, held_state

    def device_step(carried, pieces):
        rim_rows, held_state = carried
        queries, first_gate, value_rows, middle = pieces
        product = (first_gate.astype(jnp.float32) * value_rows.astype(jnp.float32)).astype(jnp.bfloat16)
        previous = jnp.concatenate([jnp.zeros((SUB - MED + 1, D), jnp.bfloat16), rim_rows, product[:TOK_DEV - SUB]], axis=0)
        sliding_spans = jnp.concatenate([previous.reshape(block_count, SUB, GROUPS, GROUP), product.reshape(block_count, SUB, GROUPS, GROUP)], axis=1)
        medium_conv = jnp.einsum("gts,bsgc->btgc", middle_filter_matrix, sliding_spans.astype(jnp.float32), precision=maximum_level).reshape(TOK_DEV, D)
        medium = medium_conv + medium_skip * product.astype(jnp.float32)
        gated_mid = (middle.astype(jnp.float32) * medium).astype(jnp.bfloat16)
        gate_product_block = gated_mid.reshape(block_count, SUB, GROUPS, GROUP).astype(jnp.float32)
        intra_part = jnp.einsum("gts,bsgc->btgc", short_filter_matrix, gate_product_block, precision=maximum_level)
        sub_states = jnp.einsum("gps,bsgc->bgpc", fold_weights, gate_product_block, precision=maximum_level)
        held_state, preceding_rows = lax.scan(sub_step, held_state, sub_states)
        previous_portion = jnp.einsum("gpt,bgpc->btgc", distance_weight, preceding_rows, precision=maximum_level)
        long_out = (intra_part + previous_portion).reshape(TOK_DEV, D) + long_skip * gated_mid.astype(jnp.float32)
        mixed = (queries.astype(jnp.float32) * long_out).astype(jnp.bfloat16)
        return (product[TOK_DEV - (MED - 1):], held_state), mixed

    start = (jnp.zeros((MED - 1, D), jnp.bfloat16), jnp.zeros((GROUPS, POLES, GROUP), jnp.float32))
    pieces = (gate_out.reshape(N_SEQ, TOK_DEV, D), gate_in.reshape(N_SEQ, TOK_DEV, D),
              values.reshape(N_SEQ, TOK_DEV, D), gate_mid.reshape(N_SEQ, TOK_DEV, D))
    _, mixed = lax.scan(device_step, start, pieces)
    return mixed.reshape(LENGTH, D)
```

```python
import functools

import jax
import jax.numpy as jnp
from jax import lax
from jax.experimental import pallas as pl
from jax.experimental.pallas import tpu as pltpu
from jax.sharding import PartitionSpec as P

SUB = 128
LANES = 128
MESH = pl.DeviceIdType.MESH
F32 = jnp.float32
BF16 = jnp.bfloat16


def iota(shape, axis):
    return lax.broadcasted_iota(jnp.int32, shape, axis)


def dot(a, b):
    return jnp.dot(a, b, preferred_element_type=F32)


def toeplitz(row):
    return pltpu.roll(jnp.broadcast_to(row, (SUB, SUB)), 0, 1, stride=1, stride_axis=0)


def kernel(
    n,
    owners,
    blocks,
    width,
    poles,
    q_hbm,
    a_hbm,
    v_hbm,
    k_hbm,
    taps_ref,
    mskip_ref,
    res_ref,
    rates_ref,
    lskip_ref,
    out_hbm,
    q_ref,
    a_ref,
    v_ref,
    k_ref,
    ext_ref,
    part_ref,
    o_ref,
    lhsm_ref,
    lhsl_ref,
    dw_ref,
    r0_ref,
    rp_ref,
    s0_ref,
    st_ref,
    gath_ref,
    cret_ref,
    cin_ref,
    in_sem,
    out_sem,
    halo_send,
    halo_recv,
    st_send,
    st_recv,
    c_send,
    c_recv,
):
    rows, features = q_hbm.shape
    tiles = features // LANES
    per_owner = tiles // owners
    chunk = per_owner * LANES
    heads = LANES // width
    half = heads // 2
    wide = blocks * LANES
    tail = rows - SUB
    me = lax.axis_index("seq")

    barrier = pltpu.get_barrier_semaphore()

    def greet(i, _):
        @pl.when(i != me)
        def _():
            pl.semaphore_signal(barrier, inc=1, device_id={"seq": i}, device_id_type=MESH)

        return 0

    lax.fori_loop(0, n, greet, 0)

    loads = [
        pltpu.make_async_copy(a_hbm.at[pl.ds(tail, SUB)], a_ref.at[pl.ds(tail, SUB)], in_sem.at[0]),
        pltpu.make_async_copy(v_hbm.at[pl.ds(tail, SUB)], v_ref.at[pl.ds(tail, SUB)], in_sem.at[1]),
        pltpu.make_async_copy(a_hbm.at[pl.ds(0, tail)], a_ref.at[pl.ds(0, tail)], in_sem.at[2]),
        pltpu.make_async_copy(v_hbm.at[pl.ds(0, tail)], v_ref.at[pl.ds(0, tail)], in_sem.at[3]),
        pltpu.make_async_copy(k_hbm, k_ref, in_sem.at[4]),
        pltpu.make_async_copy(q_hbm, q_ref, in_sem.at[5]),
    ]
    for load in loads:
        load.start()

    def lanes_of(t):
        return pl.ds(pl.multiple_of(t * LANES, LANES), LANES)

    def chunk_of(o):
        return pl.ds(pl.multiple_of(o * chunk, chunk), chunk)

    def multiply(start, count, cols):
        ext_ref[pl.ds(SUB + start, count), cols] = (
            a_ref[pl.ds(start, count), cols].astype(F32) * v_ref[pl.ds(start, count), cols].astype(F32)
        ).astype(BF16)

    def halo(o):
        return pltpu.make_async_remote_copy(
            src_ref=ext_ref.at[pl.ds(rows, SUB), chunk_of(o)],
            dst_ref=ext_ref.at[pl.ds(0, SUB), chunk_of(o)],
            send_sem=halo_send.at[o],
            recv_sem=halo_recv.at[o],
            device_id={"seq": jnp.minimum(me + 1, n - 1)},
            device_id_type=MESH,
        )

    loads[0].wait()
    loads[1].wait()
    pl.semaphore_wait(barrier, n - 1)

    def send_halo(o, _):
        multiply(tail, SUB, chunk_of(o))

        @pl.when(me < n - 1)
        def _():
            halo(o).start()

        return 0

    lax.fori_loop(0, owners, send_halo, 0)

    @pl.when(me == 0)
    def _():
        ext_ref[pl.ds(0, SUB), :] = jnp.zeros((SUB, features), BF16)

    loads[2].wait()
    loads[3].wait()

    def rest(o, _):
        multiply(0, tail, chunk_of(o))
        return 0

    lax.fori_loop(0, owners, rest, 0)

    row_id = iota((SUB, SUB), 0)
    col_id = iota((SUB, SUB), 1)
    below = col_id <= row_id
    mirror = (lax.rem(row_id + col_id, SUB) == 0).astype(BF16)
    r0_ref[...] = dot(taps_ref[...], mirror)
    head_id = iota((poles, LANES), 1) // width

    def weights(t, _):
        rate_row = rates_ref[pl.ds(t, 1), :]
        res_row = res_ref[pl.ds(t, 1), :]
        rate_col = jnp.broadcast_to(rate_row, (SUB, LANES)).T
        res_col = jnp.broadcast_to(res_row, (SUB, LANES)).T
        fold = jnp.exp(-rate_col * (SUB - 1 - col_id).astype(F32))
        rp = jnp.zeros((poles, LANES), F32)
        for g in range(heads):
            rp = jnp.where(head_id == g, rate_col[g * poles : (g + 1) * poles], rp)
        rp_ref[t] = rp
        weighted = (res_col * fold).reshape(heads, poles, SUB).sum(axis=1)
        line = pltpu.roll(weighted, 1, 1).astype(BF16).astype(F32)
        zero = jnp.zeros((SUB, SUB), F32)
        for r in range(half):
            first = jnp.where(below, toeplitz(line[r : r + 1]), zero)
            second = jnp.where(below, toeplitz(line[r + half : r + half + 1]), zero)
            lhsl_ref[t, pl.ds(r * SUB, SUB), :] = jnp.concatenate([first, second], axis=1).astype(BF16)
            lhsl_ref[t, pl.ds(half * SUB + r * poles, poles), :] = jnp.concatenate(
                [fold[r * poles : (r + 1) * poles], fold[(r + half) * poles : (r + half + 1) * poles]], axis=1
            ).astype(BF16)
        for g in range(heads):
            band = toeplitz(r0_ref[pl.ds(t * heads + g, 1), :])
            lhsm_ref[t, pl.ds(g * SUB, SUB), :] = jnp.concatenate(
                [jnp.where(below, zero, band), jnp.where(below, band, zero)], axis=1
            ).astype(BF16)
        reach = res_row * jnp.exp(-rate_row * (row_id + 1).astype(F32))
        high = reach.astype(BF16)
        dw_ref[t] = jnp.concatenate([high, (reach - high.astype(F32)).astype(BF16)], axis=1)
        return 0

    lax.fori_loop(0, tiles, weights, 0)
    loads[4].wait()

    wide_head = lax.rem(iota((SUB, wide), 1), LANES) // width
    state_head = lax.rem(iota((poles, wide), 1), LANES) // width

    def state_out(o):
        return pltpu.make_async_remote_copy(
            src_ref=st_ref.at[pl.ds(o * per_owner, per_owner)],
            dst_ref=gath_ref.at[me],
            send_sem=st_send.at[o],
            recv_sem=st_recv.at[me],
            device_id={"seq": o},
            device_id_type=MESH,
        )

    def side(ref, cols):
        return jnp.concatenate([ref[pl.ds(b * SUB, SUB), cols].astype(F32) for b in range(blocks)], axis=1)

    def main(t):
        cols = lanes_of(t)
        rhs = jnp.concatenate([ext_ref[pl.ds(b * SUB, 2 * SUB), cols] for b in range(blocks)], axis=1)
        many = dot(lhsm_ref[t], rhs)
        medium = many[:SUB]
        for g in range(1, heads):
            medium = jnp.where(wide_head == g, many[g * SUB : (g + 1) * SUB], medium)
        skip = jnp.concatenate([mskip_ref[:, cols]] * blocks, axis=1)
        medium = medium + skip * rhs[SUB:].astype(F32)
        gated = (side(k_ref, cols) * medium).astype(BF16).astype(F32)
        low = wide_head < half
        pair = jnp.concatenate([jnp.where(low, gated, 0.0), jnp.where(low, 0.0, gated)], axis=0).astype(BF16)
        many = dot(lhsl_ref[t], pair)
        inner = many[:SUB]
        base = half * SUB
        states = many[base : base + poles]
        for r in range(1, half):
            inner = jnp.where(lax.rem(wide_head, half) == r, many[r * SUB : (r + 1) * SUB], inner)
            states = jnp.where(
                lax.rem(state_head, half) == r, many[base + r * poles : base + (r + 1) * poles], states
            )
        inner = inner + jnp.concatenate([lskip_ref[:, cols]] * blocks, axis=1) * gated
        decay = jnp.exp(rp_ref[t] * (-1.0 * SUB))
        held = jnp.zeros((poles, LANES), F32)
        for b in range(blocks):
            part_ref[pl.ds(b * SUB, SUB), cols] = inner[:, b * LANES : (b + 1) * LANES]
            s0_ref[t, b] = held
            held = decay * held + states[:, b * LANES : (b + 1) * LANES]
        st_ref[t] = held

    def work(o, _):
        @pl.when(me > 0)
        def _():
            halo(o).wait_recv()

        for k in range(per_owner):
            main(o * per_owner + k)

        @pl.when(o != me)
        def _():
            state_out(o).start()

        return 0

    lax.fori_loop(0, owners, work, 0)

    def carry_back(e):
        return pltpu.make_async_remote_copy(
            src_ref=cret_ref.at[e],
            dst_ref=cin_ref.at[pl.ds(me * per_owner, per_owner)],
            send_sem=c_send.at[e],
            recv_sem=c_recv.at[me],
            device_id={"seq": e},
            device_id_type=MESH,
        )

    def state_in(e):
        return pltpu.make_async_remote_copy(
            src_ref=st_ref.at[pl.ds(0, per_owner)],
            dst_ref=gath_ref.at[e],
            send_sem=st_send.at[0],
            recv_sem=st_recv.at[e],
            device_id={"seq": e},
            device_id_type=MESH,
        )

    def carry_in(o):
        return pltpu.make_async_remote_copy(
            src_ref=cret_ref.at[0],
            dst_ref=cin_ref.at[pl.ds(o * per_owner, per_owner)],
            send_sem=c_send.at[0],
            recv_sem=c_recv.at[o],
            device_id={"seq": o},
            device_id_type=MESH,
        )

    @pl.when(me < owners)
    def _():
        mine = pl.ds(me * per_owner, per_owner)
        gath_ref[me] = st_ref[mine]
        power = jnp.exp(rp_ref[mine] * (-1.0 * SUB * blocks))

        def scan(e, held):
            cret_ref[e] = held

            @pl.when(e != me)
            def _():
                carry_back(e).start()
                state_in(e).wait_recv()

            return power * held + gath_ref[e]

        lax.fori_loop(0, n, scan, jnp.zeros((per_owner, poles, LANES), F32))
        cin_ref[mine] = cret_ref[me]

    loads[5].wait()

    def result(o):
        return pltpu.make_async_copy(o_ref.at[:, chunk_of(o)], out_hbm.at[:, chunk_of(o)], out_sem.at[o])

    spot = iota((heads * poles, wide), 0) // poles == lax.rem(iota((heads * poles, wide), 1), LANES) // width

    def finish(t):
        cols = lanes_of(t)
        decay = jnp.exp(rp_ref[t] * (-1.0 * SUB))
        carried = cin_ref[t]
        before = []
        for b in range(blocks):
            before.append(carried + s0_ref[t, b])
            carried = decay * carried
        before = jnp.concatenate(before, axis=1)
        spread = jnp.where(spot, jnp.concatenate([before] * heads, axis=0), 0.0)
        high = spread.astype(BF16)
        low = (spread - high.astype(F32)).astype(BF16)
        reach = dot(dw_ref[t], jnp.concatenate([high, high], axis=0)) + dot(dw_ref[t, :, : heads * poles], low)
        for b in range(blocks):
            at = pl.ds(b * SUB, SUB)
            o_ref[at, cols] = (
                q_ref[at, cols].astype(F32) * (part_ref[at, cols] + reach[:, b * LANES : (b + 1) * LANES])
            ).astype(BF16)

    def closing(o, _):
        @pl.when(o != me)
        def _():
            carry_in(o).wait_recv()

        for k in range(per_owner):
            finish(o * per_owner + k)
        result(o).start()
        return 0

    lax.fori_loop(0, owners, closing, 0)

    def drain(o, _):
        result(o).wait()

        @pl.when(o != me)
        def _():
            state_out(o).wait_send()

        @pl.when(me < n - 1)
        def _():
            halo(o).wait_send()

        return 0

    lax.fori_loop(0, owners, drain, 0)

    @pl.when(me < owners)
    def _():
        def drain_carry(e, _):
            @pl.when(e != me)
            def _():
                carry_back(e).wait_send()

            return 0

        lax.fori_loop(0, n, drain_carry, 0)


def shards(
    gate_out, gate_in, values, gate_mid, medium_taps, medium_skip, residues, rates, long_skip
):
    rows, features = gate_out.shape
    groups, poles = rates.shape
    width = features // groups
    blocks = rows // SUB
    tiles = features // LANES
    n = lax.axis_size("seq")
    owners = min(n, tiles)
    per_owner = tiles // owners
    heads = LANES // width
    stripe = (rows, features)
    vmem = pl.BlockSpec(memory_space=pltpu.VMEM)
    hbm = pl.BlockSpec(memory_space=pl.ANY)
    flops = 2 * tiles * SUB * 2 * SUB * blocks * LANES * (heads + heads // 2 + 2)
    return pl.pallas_call(
        functools.partial(kernel, n, owners, blocks, width, poles),
        out_shape=jax.ShapeDtypeStruct(stripe, BF16),
        in_specs=[hbm] * 4 + [vmem] * 5,
        out_specs=hbm,
        scratch_shapes=[
            pltpu.VMEM(stripe, BF16),
            pltpu.VMEM(stripe, BF16),
            pltpu.VMEM(stripe, BF16),
            pltpu.VMEM(stripe, BF16),
            pltpu.VMEM((rows + SUB, features), BF16),
            pltpu.VMEM(stripe, F32),
            pltpu.VMEM(stripe, BF16),
            pltpu.VMEM((tiles, heads * SUB, 2 * SUB), BF16),
            pltpu.VMEM((tiles, heads // 2 * (SUB + poles), 2 * SUB), BF16),
            pltpu.VMEM((tiles, SUB, 2 * heads * poles), BF16),
            pltpu.VMEM((groups, SUB), F32),
            pltpu.VMEM((tiles, poles, LANES), F32),
            pltpu.VMEM((tiles, blocks, poles, LANES), F32),
            pltpu.VMEM((tiles, poles, LANES), F32),
            pltpu.VMEM((n, per_owner, poles, LANES), F32),
            pltpu.VMEM((n, per_owner, poles, LANES), F32),
            pltpu.VMEM((tiles, poles, LANES), F32),
            pltpu.SemaphoreType.DMA((6,)),
            pltpu.SemaphoreType.DMA((owners,)),
            pltpu.SemaphoreType.DMA((owners,)),
            pltpu.SemaphoreType.DMA((owners,)),
            pltpu.SemaphoreType.DMA((owners,)),
            pltpu.SemaphoreType.DMA((n,)),
            pltpu.SemaphoreType.DMA((n,)),
            pltpu.SemaphoreType.DMA((owners,)),
        ],
        compiler_params=pltpu.CompilerParams(
            collective_id=0, has_side_effects=True, vmem_limit_bytes=60 * 1024 * 1024
        ),
        cost_estimate=pl.CostEstimate(flops=flops, bytes_accessed=10 * rows * features, transcendentals=0),
    )(
        gate_out,
        gate_in,
        values,
        gate_mid,
        medium_taps,
        medium_skip.reshape(1, features),
        residues.reshape(tiles, heads * poles),
        rates.reshape(tiles, heads * poles),
        long_skip.reshape(1, features),
    )


def solution(mesh):
    rows = P(("grp", "seq"), None)
    in_specs = (rows, rows, rows, rows, P(), P(), P(), P(), P())
    return jax.shard_map(shards, mesh=mesh, in_specs=in_specs, out_specs=rows, check_vma=False)
```

```python
import functools

import jax
import jax.numpy as jnp
from jax import lax
from jax.experimental import pallas as pl
from jax.experimental.pallas import tpu as pltpu
from jax.sharding import PartitionSpec as P

SUB = 128
LANES = 128
STRIP = 16
MESH = pl.DeviceIdType.MESH
F32 = jnp.float32
BF16 = jnp.bfloat16


def iota(shape, axis):
    return lax.broadcasted_iota(jnp.int32, shape, axis)


def dot(a, b):
    return jnp.dot(a, b, preferred_element_type=F32)


def toeplitz(row):
    strip = jnp.broadcast_to(row, (STRIP, SUB))
    strip = pltpu.roll(strip, 0, 1, stride=1, stride_axis=0).astype(BF16)
    return jnp.concatenate([strip] + [pltpu.roll(strip, k, 1) for k in range(STRIP, SUB, STRIP)], axis=0)


def thirds(x):
    high = x.astype(BF16)
    rest = x - high.astype(F32)
    middle = rest.astype(BF16)
    return [high, middle, (rest - middle.astype(F32)).astype(BF16)]


def kernel(
    n,
    owners,
    blocks,
    width,
    poles,
    q_hbm,
    a_hbm,
    v_hbm,
    k_hbm,
    taps_ref,
    mskip_ref,
    res_ref,
    rates_ref,
    lskip_ref,
    out_hbm,
    q_ref,
    a_ref,
    v_ref,
    k_ref,
    ext_ref,
    part_ref,
    o_ref,
    lhsm_ref,
    lhsl_ref,
    dw_ref,
    r0_ref,
    rp_ref,
    s0_ref,
    st_ref,
    gath_ref,
    cret_ref,
    cin_ref,
    in_sem,
    out_sem,
    halo_send,
    halo_recv,
    st_send,
    st_recv,
    c_send,
    c_recv,
):
    rows, features = q_hbm.shape
    tiles = features // LANES
    per_owner = tiles // owners
    chunk = per_owner * LANES
    heads = LANES // width
    half = heads // 2
    wide = blocks * LANES
    tail = rows - SUB
    me = lax.axis_index("seq")

    barrier = pltpu.get_barrier_semaphore()

    def greet(i, _):
        @pl.when(i != me)
        def _():
            pl.semaphore_signal(barrier, inc=1, device_id={"seq": i}, device_id_type=MESH)

        return 0

    lax.fori_loop(0, n, greet, 0)

    loads = [
        pltpu.make_async_copy(a_hbm.at[pl.ds(tail, SUB)], a_ref.at[pl.ds(tail, SUB)], in_sem.at[0]),
        pltpu.make_async_copy(v_hbm.at[pl.ds(tail, SUB)], v_ref.at[pl.ds(tail, SUB)], in_sem.at[1]),
        pltpu.make_async_copy(a_hbm.at[pl.ds(0, tail)], a_ref.at[pl.ds(0, tail)], in_sem.at[2]),
        pltpu.make_async_copy(v_hbm.at[pl.ds(0, tail)], v_ref.at[pl.ds(0, tail)], in_sem.at[3]),
        pltpu.make_async_copy(k_hbm, k_ref, in_sem.at[4]),
        pltpu.make_async_copy(q_hbm, q_ref, in_sem.at[5]),
    ]
    for load in loads:
        load.start()

    def lanes_of(t):
        return pl.ds(pl.multiple_of(t * LANES, LANES), LANES)

    def chunk_of(o):
        return pl.ds(pl.multiple_of(o * chunk, chunk), chunk)

    def multiply(start, count, cols):
        ext_ref[pl.ds(SUB + start, count), cols] = (
            a_ref[pl.ds(start, count), cols].astype(F32) * v_ref[pl.ds(start, count), cols].astype(F32)
        ).astype(BF16)

    def halo(o):
        return pltpu.make_async_remote_copy(
            src_ref=ext_ref.at[pl.ds(rows, SUB), chunk_of(o)],
            dst_ref=ext_ref.at[pl.ds(0, SUB), chunk_of(o)],
            send_sem=halo_send.at[o],
            recv_sem=halo_recv.at[o],
            device_id={"seq": jnp.minimum(me + 1, n - 1)},
            device_id_type=MESH,
        )

    loads[0].wait()
    loads[1].wait()
    pl.semaphore_wait(barrier, n - 1)

    def send_halo(i, _):
        o = lax.rem(me + 1 + i, owners)
        multiply(tail, SUB, chunk_of(o))

        @pl.when(me < n - 1)
        def _():
            halo(o).start()

        return 0

    lax.fori_loop(0, owners, send_halo, 0)

    @pl.when(me == 0)
    def _():
        ext_ref[pl.ds(0, SUB), :] = jnp.zeros((SUB, features), BF16)

    loads[2].wait()
    loads[3].wait()

    def rest(o, _):
        multiply(0, tail, chunk_of(o))
        return 0

    lax.fori_loop(0, owners, rest, 0)

    row_id = iota((SUB, SUB), 0)
    col_id = iota((SUB, SUB), 1)
    below = (col_id <= row_id).astype(F32).astype(BF16)
    mirror = (lax.rem(row_id + col_id, SUB) == 0).astype(BF16)
    r0_ref[...] = dot(taps_ref[...], mirror)
    table = jnp.concatenate(thirds(rates_ref[...]) + thirds(res_ref[...]), axis=0)
    groups = rates_ref.shape[1]
    pick_row, pick_col = iota((groups, LANES), 0), iota((groups, LANES), 1) // width

    def weights(t):
        spread = dot(table, (pick_row == t * heads + pick_col).astype(F32).astype(BF16))
        spread = [spread[k * poles : (k + 1) * poles] for k in range(6)]
        rp = spread[0] + spread[1] + spread[2]
        sp = spread[3] + spread[4] + spread[5]
        rp_ref[t] = rp

        def column(x):
            return jnp.concatenate(
                [jnp.broadcast_to(x[:, g * width : g * width + 1], (poles, LANES)) for g in range(heads)], axis=0
            )

        rate_col, res_col = column(rp), column(sp)
        fold = jnp.exp(-rate_col * (SUB - 1 - col_id).astype(F32))
        weighted = (res_col * fold).reshape(heads, poles, SUB).sum(axis=1)
        line = pltpu.roll(weighted, 1, 1).astype(BF16).astype(F32)
        for r in range(half):
            first = toeplitz(line[r : r + 1]) * below
            second = toeplitz(line[r + half : r + half + 1]) * below
            lhsl_ref[t, pl.ds(r * SUB, SUB), :] = jnp.concatenate([first, second], axis=1)
            lhsl_ref[t, pl.ds(half * SUB + r * poles, poles), :] = jnp.concatenate(
                [fold[r * poles : (r + 1) * poles], fold[(r + half) * poles : (r + half + 1) * poles]], axis=1
            ).astype(BF16)
        for g in range(heads):
            band = toeplitz(r0_ref[pl.ds(t * heads + g, 1), :])
            now = band * below
            lhsm_ref[t, pl.ds(g * SUB, SUB), :] = jnp.concatenate([band - now, now], axis=1)
        reach = (res_col * jnp.exp(-rate_col * (col_id + 1).astype(F32))).T
        high = reach.astype(BF16)
        dw_ref[t] = jnp.concatenate([high, (reach - high.astype(F32)).astype(BF16)], axis=1)

    def weights_of(o, _):
        for k in range(per_owner):
            weights(o * per_owner + k)
        return 0

    lax.fori_loop(0, owners, weights_of, 0)
    loads[4].wait()

    wide_head = lax.rem(iota((SUB, wide), 1), LANES) // width
    state_head = lax.rem(iota((poles, wide), 1), LANES) // width

    def state_out(o):
        return pltpu.make_async_remote_copy(
            src_ref=st_ref.at[pl.ds(o * per_owner, per_owner)],
            dst_ref=gath_ref.at[me],
            send_sem=st_send.at[o],
            recv_sem=st_recv.at[me],
            device_id={"seq": o},
            device_id_type=MESH,
        )

    def side(ref, cols):
        return jnp.concatenate([ref[pl.ds(b * SUB, SUB), cols].astype(F32) for b in range(blocks)], axis=1)

    def main(t):
        cols = lanes_of(t)
        rhs = jnp.concatenate([ext_ref[pl.ds(b * SUB, 2 * SUB), cols] for b in range(blocks)], axis=1)
        many = dot(lhsm_ref[t], rhs)
        medium = many[:SUB]
        for g in range(1, heads):
            medium = jnp.where(wide_head == g, many[g * SUB : (g + 1) * SUB], medium)
        skip = jnp.concatenate([mskip_ref[:, cols]] * blocks, axis=1)
        medium = medium + skip * rhs[SUB:].astype(F32)
        gated = (side(k_ref, cols) * medium).astype(BF16).astype(F32)
        low = wide_head < half
        pair = jnp.concatenate([jnp.where(low, gated, 0.0), jnp.where(low, 0.0, gated)], axis=0).astype(BF16)
        many = dot(lhsl_ref[t], pair)
        inner = many[:SUB]
        base = half * SUB
        states = many[base : base + poles]
        for r in range(1, half):
            inner = jnp.where(lax.rem(wide_head, half) == r, many[r * SUB : (r + 1) * SUB], inner)
            states = jnp.where(
                lax.rem(state_head, half) == r, many[base + r * poles : base + (r + 1) * poles], states
            )
        inner = inner + jnp.concatenate([lskip_ref[:, cols]] * blocks, axis=1) * gated
        decay = jnp.exp(rp_ref[t] * (-1.0 * SUB))
        held = jnp.zeros((poles, LANES), F32)
        for b in range(blocks):
            part_ref[pl.ds(b * SUB, SUB), cols] = inner[:, b * LANES : (b + 1) * LANES]
            s0_ref[t, b] = held
            held = decay * held + states[:, b * LANES : (b + 1) * LANES]
        st_ref[t] = held

    def work(i, _):
        o = lax.rem(me + i, owners)

        @pl.when(me > 0)
        def _():
            halo(o).wait_recv()

        for k in range(per_owner):
            main(o * per_owner + k)

        @pl.when(o != me)
        def _():
            state_out(o).start()

        return 0

    lax.fori_loop(0, owners, work, 0)

    def carry_back(e):
        return pltpu.make_async_remote_copy(
            src_ref=cret_ref.at[e],
            dst_ref=cin_ref.at[pl.ds(me * per_owner, per_owner)],
            send_sem=c_send.at[e],
            recv_sem=c_recv.at[me],
            device_id={"seq": e},
            device_id_type=MESH,
        )

    def state_in(e):
        return pltpu.make_async_remote_copy(
            src_ref=st_ref.at[pl.ds(0, per_owner)],
            dst_ref=gath_ref.at[e],
            send_sem=st_send.at[0],
            recv_sem=st_recv.at[e],
            device_id={"seq": e},
            device_id_type=MESH,
        )

    def carry_in(o):
        return pltpu.make_async_remote_copy(
            src_ref=cret_ref.at[0],
            dst_ref=cin_ref.at[pl.ds(o * per_owner, per_owner)],
            send_sem=c_send.at[0],
            recv_sem=c_recv.at[o],
            device_id={"seq": o},
            device_id_type=MESH,
        )

    @pl.when(me < owners)
    def _():
        mine = pl.ds(me * per_owner, per_owner)
        gath_ref[me] = st_ref[mine]
        power = jnp.exp(rp_ref[mine] * (-1.0 * SUB * blocks))

        def scan(e, held):
            cret_ref[e] = held.astype(BF16)

            @pl.when(e != me)
            def _():
                state_in(e).wait_recv()

            return power * held + gath_ref[e]

        lax.fori_loop(0, n, scan, jnp.zeros((per_owner, poles, LANES), F32))

        def give(i, _):
            carry_back(lax.rem(me + i, n)).start()
            return 0

        lax.fori_loop(1, n, give, 0)
        cin_ref[mine] = cret_ref[me]

    loads[5].wait()

    def result(o):
        return pltpu.make_async_copy(o_ref.at[:, chunk_of(o)], out_hbm.at[:, chunk_of(o)], out_sem.at[o])

    spot = iota((heads * poles, wide), 0) // poles == lax.rem(iota((heads * poles, wide), 1), LANES) // width

    def finish(t):
        cols = lanes_of(t)
        decay = jnp.exp(rp_ref[t] * (-1.0 * SUB))
        carried = cin_ref[t].astype(F32)
        before = []
        for b in range(blocks):
            before.append(carried + s0_ref[t, b])
            carried = decay * carried
        before = jnp.concatenate(before, axis=1)
        spread = jnp.where(spot, jnp.concatenate([before] * heads, axis=0), 0.0)
        high = spread.astype(BF16)
        low = (spread - high.astype(F32)).astype(BF16)
        reach = dot(dw_ref[t], jnp.concatenate([high, high], axis=0)) + dot(dw_ref[t, :, : heads * poles], low)
        for b in range(blocks):
            at = pl.ds(b * SUB, SUB)
            o_ref[at, cols] = (
                q_ref[at, cols].astype(F32) * (part_ref[at, cols] + reach[:, b * LANES : (b + 1) * LANES])
            ).astype(BF16)

    def closing(i, _):
        o = lax.rem(me + owners - i, owners) if n == owners else i

        @pl.when(o != me)
        def _():
            carry_in(o).wait_recv()

        for k in range(per_owner):
            finish(o * per_owner + k)
        result(o).start()
        return 0

    lax.fori_loop(0, owners, closing, 0)

    def drain(o, _):
        result(o).wait()

        @pl.when(o != me)
        def _():
            state_out(o).wait_send()

        @pl.when(me < n - 1)
        def _():
            halo(o).wait_send()

        return 0

    lax.fori_loop(0, owners, drain, 0)

    @pl.when(me < owners)
    def _():
        def drain_carry(e, _):
            @pl.when(e != me)
            def _():
                carry_back(e).wait_send()

            return 0

        lax.fori_loop(0, n, drain_carry, 0)


def shards(
    gate_out, gate_in, values, gate_mid, medium_taps, medium_skip, residues, rates, long_skip
):
    rows, features = gate_out.shape
    groups, poles = rates.shape
    width = features // groups
    blocks = rows // SUB
    tiles = features // LANES
    n = lax.axis_size("seq")
    owners = min(n, tiles)
    per_owner = tiles // owners
    heads = LANES // width
    stripe = (rows, features)
    vmem = pl.BlockSpec(memory_space=pltpu.VMEM)
    hbm = pl.BlockSpec(memory_space=pl.ANY)
    flops = 2 * tiles * SUB * 2 * SUB * blocks * LANES * (heads + heads // 2 + 2)
    return pl.pallas_call(
        functools.partial(kernel, n, owners, blocks, width, poles),
        out_shape=jax.ShapeDtypeStruct(stripe, BF16),
        in_specs=[hbm] * 4 + [vmem] * 5,
        out_specs=hbm,
        scratch_shapes=[
            pltpu.VMEM(stripe, BF16),
            pltpu.VMEM(stripe, BF16),
            pltpu.VMEM(stripe, BF16),
            pltpu.VMEM(stripe, BF16),
            pltpu.VMEM((rows + SUB, features), BF16),
            pltpu.VMEM(stripe, F32),
            pltpu.VMEM(stripe, BF16),
            pltpu.VMEM((tiles, heads * SUB, 2 * SUB), BF16),
            pltpu.VMEM((tiles, heads // 2 * (SUB + poles), 2 * SUB), BF16),
            pltpu.VMEM((tiles, SUB, 2 * heads * poles), BF16),
            pltpu.VMEM((groups, SUB), F32),
            pltpu.VMEM((tiles, poles, LANES), F32),
            pltpu.VMEM((tiles, blocks, poles, LANES), F32),
            pltpu.VMEM((tiles, poles, LANES), F32),
            pltpu.VMEM((n, per_owner, poles, LANES), F32),
            pltpu.VMEM((n, per_owner, poles, LANES), BF16),
            pltpu.VMEM((tiles, poles, LANES), BF16),
            pltpu.SemaphoreType.DMA((6,)),
            pltpu.SemaphoreType.DMA((owners,)),
            pltpu.SemaphoreType.DMA((owners,)),
            pltpu.SemaphoreType.DMA((owners,)),
            pltpu.SemaphoreType.DMA((owners,)),
            pltpu.SemaphoreType.DMA((n,)),
            pltpu.SemaphoreType.DMA((n,)),
            pltpu.SemaphoreType.DMA((owners,)),
        ],
        compiler_params=pltpu.CompilerParams(
            collective_id=0, has_side_effects=True, vmem_limit_bytes=60 * 1024 * 1024
        ),
        cost_estimate=pl.CostEstimate(flops=flops, bytes_accessed=10 * rows * features, transcendentals=0),
    )(
        gate_out,
        gate_in,
        values,
        gate_mid,
        medium_taps,
        medium_skip.reshape(1, features),
        residues.T,
        rates.T,
        long_skip.reshape(1, features),
    )


def solution(mesh):
    rows = P(("grp", "seq"), None)
    in_specs = (rows, rows, rows, rows, P(), P(), P(), P(), P())
    return jax.shard_map(shards, mesh=mesh, in_specs=in_specs, out_specs=rows, check_vma=False)
```

```python
import functools

import jax
import jax.numpy as jnp
from jax import lax
from jax.experimental import pallas as pl
from jax.experimental.pallas import tpu as pltpu
from jax.sharding import PartitionSpec as P

SUB = 128
LANES = 128
STRIP = 32
MESH = pl.DeviceIdType.MESH
F32 = jnp.float32
BF16 = jnp.bfloat16


def iota(shape, axis):
    return lax.broadcasted_iota(jnp.int32, shape, axis)


def dot(a, b):
    return jnp.dot(a, b, preferred_element_type=F32)


def toeplitz(row, shift):
    return pltpu.roll(jnp.broadcast_to(row, (STRIP, SUB)), shift, 1, stride=1, stride_axis=0)


def thirds(x):
    high = x.astype(BF16)
    rest = x - high.astype(F32)
    middle = rest.astype(BF16)
    return [high, middle, (rest - middle.astype(F32)).astype(BF16)]


def kernel(
    n,
    owners,
    blocks,
    width,
    poles,
    q_hbm,
    a_hbm,
    v_hbm,
    k_hbm,
    taps_ref,
    mskip_ref,
    res_ref,
    rates_ref,
    lskip_ref,
    out_hbm,
    q_ref,
    a_ref,
    v_ref,
    k_ref,
    ext_ref,
    part_ref,
    o_ref,
    lhsm_ref,
    lhsl_ref,
    dw_ref,
    r0_ref,
    rp_ref,
    s0_ref,
    st_ref,
    gath_ref,
    cret_ref,
    cin_ref,
    in_sem,
    out_sem,
    halo_send,
    halo_recv,
    st_send,
    st_recv,
    c_send,
    c_recv,
):
    rows, features = q_hbm.shape
    tiles = features // LANES
    per_owner = tiles // owners
    chunk = per_owner * LANES
    heads = LANES // width
    half = heads // 2
    wide = blocks * LANES
    tail = rows - SUB
    me = lax.axis_index("seq")

    barrier = pltpu.get_barrier_semaphore()

    def greet(i, _):
        @pl.when(i != me)
        def _():
            pl.semaphore_signal(barrier, inc=1, device_id={"seq": i}, device_id_type=MESH)

        return 0

    lax.fori_loop(0, n, greet, 0)

    loads = [
        pltpu.make_async_copy(a_hbm.at[pl.ds(tail, SUB)], a_ref.at[pl.ds(tail, SUB)], in_sem.at[0]),
        pltpu.make_async_copy(v_hbm.at[pl.ds(tail, SUB)], v_ref.at[pl.ds(tail, SUB)], in_sem.at[1]),
        pltpu.make_async_copy(a_hbm.at[pl.ds(0, tail)], a_ref.at[pl.ds(0, tail)], in_sem.at[2]),
        pltpu.make_async_copy(v_hbm.at[pl.ds(0, tail)], v_ref.at[pl.ds(0, tail)], in_sem.at[3]),
        pltpu.make_async_copy(k_hbm, k_ref, in_sem.at[4]),
        pltpu.make_async_copy(q_hbm, q_ref, in_sem.at[5]),
    ]
    for load in loads:
        load.start()

    def lanes_of(t):
        return pl.ds(pl.multiple_of(t * LANES, LANES), LANES)

    def chunk_of(o):
        return pl.ds(pl.multiple_of(o * chunk, chunk), chunk)

    def multiply(start, count, cols):
        ext_ref[pl.ds(SUB + start, count), cols] = (
            a_ref[pl.ds(start, count), cols].astype(F32) * v_ref[pl.ds(start, count), cols].astype(F32)
        ).astype(BF16)

    def halo(o):
        return pltpu.make_async_remote_copy(
            src_ref=ext_ref.at[pl.ds(rows, SUB), chunk_of(o)],
            dst_ref=ext_ref.at[pl.ds(0, SUB), chunk_of(o)],
            send_sem=halo_send.at[o],
            recv_sem=halo_recv.at[o],
            device_id={"seq": jnp.minimum(me + 1, n - 1)},
            device_id_type=MESH,
        )

    loads[0].wait()
    loads[1].wait()
    pl.semaphore_wait(barrier, n - 1)

    def send_halo(i, _):
        o = lax.rem(me + 1 + i, owners)
        multiply(tail, SUB, chunk_of(o))

        @pl.when(me < n - 1)
        def _():
            halo(o).start()

        return 0

    lax.fori_loop(0, owners, send_halo, 0)

    @pl.when(me == 0)
    def _():
        ext_ref[pl.ds(0, SUB), :] = jnp.zeros((SUB, features), BF16)

    loads[2].wait()
    loads[3].wait()

    def rest(o, _):
        multiply(0, tail, chunk_of(o))
        return 0

    lax.fori_loop(0, owners, rest, 0)

    row_id = iota((SUB, SUB), 0)
    col_id = iota((SUB, SUB), 1)
    strip_row, strip_col = iota((STRIP, SUB), 0), iota((STRIP, SUB), 1)
    below = strip_col <= strip_row
    inside = strip_col <= strip_row + (SUB - STRIP)
    zero = jnp.zeros((STRIP, SUB), F32)
    mirror = (lax.rem(row_id + col_id, SUB) == 0).astype(BF16)
    r0_ref[...] = dot(taps_ref[...], mirror)
    table = jnp.concatenate(thirds(rates_ref[...]) + thirds(res_ref[...]), axis=0)
    groups = rates_ref.shape[1]
    pick_row, pick_col = iota((groups, LANES), 0), iota((groups, LANES), 1) // width

    def weights(t):
        spread = dot(table, (pick_row == t * heads + pick_col).astype(F32).astype(BF16))
        spread = [spread[k * poles : (k + 1) * poles] for k in range(6)]
        rp = spread[0] + spread[1] + spread[2]
        sp = spread[3] + spread[4] + spread[5]
        rp_ref[t] = rp

        def column(x):
            return jnp.concatenate(
                [jnp.broadcast_to(x[:, g * width : g * width + 1], (poles, LANES)) for g in range(heads)], axis=0
            )

        rate_col, res_col = column(rp), column(sp)
        fold = jnp.exp(-rate_col * (SUB - 1 - col_id).astype(F32))
        weighted = (res_col * fold).reshape(heads, poles, SUB).sum(axis=1)
        line = pltpu.roll(weighted, 1, 1).astype(BF16).astype(F32)
        for r in range(half):
            first = jnp.where(inside, toeplitz(line[r : r + 1], SUB - STRIP), zero)
            second = jnp.where(inside, toeplitz(line[r + half : r + half + 1], SUB - STRIP), zero)
            lhsl_ref[t, pl.ds(r * STRIP, STRIP), :] = jnp.concatenate([first, second], axis=1).astype(BF16)
            lhsl_ref[t, pl.ds(half * STRIP + r * poles, poles), :] = jnp.concatenate(
                [fold[r * poles : (r + 1) * poles], fold[(r + half) * poles : (r + half + 1) * poles]], axis=1
            ).astype(BF16)
        for g in range(heads):
            band = toeplitz(r0_ref[pl.ds(t * heads + g, 1), :], 0)
            lhsm_ref[t, pl.ds(g * STRIP, STRIP), :] = jnp.concatenate(
                [jnp.where(below, zero, band), jnp.where(below, band, zero)], axis=1
            ).astype(BF16)
        reach = (res_col * jnp.exp(-rate_col * (col_id + 1).astype(F32))).T
        high = reach.astype(BF16)
        dw_ref[t] = jnp.concatenate([high, (reach - high.astype(F32)).astype(BF16)], axis=1)

    def weights_of(o, _):
        for k in range(per_owner):
            weights(o * per_owner + k)
        return 0

    lax.fori_loop(0, owners, weights_of, 0)
    loads[4].wait()

    strip_head = lax.rem(iota((STRIP, wide), 1), LANES) // width
    state_head = lax.rem(iota((poles, wide), 1), LANES) // width
    low = lax.rem(iota((SUB, wide), 1), LANES) // width < half

    def state_out(o):
        return pltpu.make_async_remote_copy(
            src_ref=st_ref.at[pl.ds(o * per_owner, per_owner)],
            dst_ref=gath_ref.at[me],
            send_sem=st_send.at[o],
            recv_sem=st_recv.at[me],
            device_id={"seq": o},
            device_id_type=MESH,
        )

    def side(ref, cols):
        return jnp.concatenate([ref[pl.ds(b * SUB, SUB), cols].astype(F32) for b in range(blocks)], axis=1)

    def main(t):
        cols = lanes_of(t)
        reach = SUB + STRIP
        medium = []
        for start in range(0, SUB, STRIP):
            rhs = jnp.concatenate([ext_ref[pl.ds(b * SUB + start, reach), cols] for b in range(blocks)], axis=1)
            many = dot(lhsm_ref[t, :, :reach], rhs)
            strip = many[:STRIP]
            for g in range(1, heads):
                strip = jnp.where(strip_head == g, many[g * STRIP : (g + 1) * STRIP], strip)
            medium.append(strip)
        medium = jnp.concatenate(medium, axis=0)
        product = jnp.concatenate([ext_ref[pl.ds((b + 1) * SUB, SUB), cols] for b in range(blocks)], axis=1)
        skip = jnp.concatenate([mskip_ref[:, cols]] * blocks, axis=1)
        medium = medium + skip * product.astype(F32)
        gated = (side(k_ref, cols) * medium).astype(BF16).astype(F32)
        pad = jnp.zeros((SUB - STRIP, wide), BF16)
        first = jnp.concatenate([pad, jnp.where(low, gated, 0.0).astype(BF16)], axis=0)
        second = jnp.concatenate([pad, jnp.where(low, 0.0, gated).astype(BF16)], axis=0)
        inner = []
        for start in range(0, SUB, STRIP):
            pair = jnp.concatenate([first[start : start + SUB], second[start : start + SUB]], axis=0)
            last = start + STRIP == SUB
            many = dot(lhsl_ref[t] if last else lhsl_ref[t, : half * STRIP], pair)
            strip = many[:STRIP]
            for r in range(1, half):
                strip = jnp.where(lax.rem(strip_head, half) == r, many[r * STRIP : (r + 1) * STRIP], strip)
            inner.append(strip)
        inner = jnp.concatenate(inner, axis=0)
        base = half * STRIP
        states = many[base : base + poles]
        for r in range(1, half):
            states = jnp.where(
                lax.rem(state_head, half) == r, many[base + r * poles : base + (r + 1) * poles], states
            )
        inner = inner + jnp.concatenate([lskip_ref[:, cols]] * blocks, axis=1) * gated
        decay = jnp.exp(rp_ref[t] * (-1.0 * SUB))
        held = jnp.zeros((poles, LANES), F32)
        for b in range(blocks):
            part_ref[pl.ds(b * SUB, SUB), cols] = inner[:, b * LANES : (b + 1) * LANES]
            s0_ref[t, b] = held
            held = decay * held + states[:, b * LANES : (b + 1) * LANES]
        st_ref[t] = held

    def work(i, _):
        o = lax.rem(me + i, owners)

        @pl.when(me > 0)
        def _():
            halo(o).wait_recv()

        for k in range(per_owner):
            main(o * per_owner + k)

        @pl.when(o != me)
        def _():
            state_out(o).start()

        return 0

    lax.fori_loop(0, owners, work, 0)

    def carry_back(e):
        return pltpu.make_async_remote_copy(
            src_ref=cret_ref.at[e],
            dst_ref=cin_ref.at[pl.ds(me * per_owner, per_owner)],
            send_sem=c_send.at[e],
            recv_sem=c_recv.at[me],
            device_id={"seq": e},
            device_id_type=MESH,
        )

    def state_in(e):
        return pltpu.make_async_remote_copy(
            src_ref=st_ref.at[pl.ds(0, per_owner)],
            dst_ref=gath_ref.at[e],
            send_sem=st_send.at[0],
            recv_sem=st_recv.at[e],
            device_id={"seq": e},
            device_id_type=MESH,
        )

    def carry_in(o):
        return pltpu.make_async_remote_copy(
            src_ref=cret_ref.at[0],
            dst_ref=cin_ref.at[pl.ds(o * per_owner, per_owner)],
            send_sem=c_send.at[0],
            recv_sem=c_recv.at[o],
            device_id={"seq": o},
            device_id_type=MESH,
        )

    @pl.when(me < owners)
    def _():
        mine = pl.ds(me * per_owner, per_owner)
        gath_ref[me] = st_ref[mine]
        power = jnp.exp(rp_ref[mine] * (-1.0 * SUB * blocks))

        def scan(e, held):
            cret_ref[e] = held.astype(BF16)

            @pl.when(e != me)
            def _():
                state_in(e).wait_recv()

            return power * held + gath_ref[e]

        lax.fori_loop(0, n, scan, jnp.zeros((per_owner, poles, LANES), F32))

        def give(i, _):
            carry_back(lax.rem(me + i, n)).start()
            return 0

        lax.fori_loop(1, n, give, 0)
        cin_ref[mine] = cret_ref[me]

    loads[5].wait()

    def result(o):
        return pltpu.make_async_copy(o_ref.at[:, chunk_of(o)], out_hbm.at[:, chunk_of(o)], out_sem.at[o])

    spot = iota((heads * poles, wide), 0) // poles == lax.rem(iota((heads * poles, wide), 1), LANES) // width

    def finish(t):
        cols = lanes_of(t)
        decay = jnp.exp(rp_ref[t] * (-1.0 * SUB))
        carried = cin_ref[t].astype(F32)
        before = []
        for b in range(blocks):
            before.append(carried + s0_ref[t, b])
            carried = decay * carried
        before = jnp.concatenate(before, axis=1)
        spread = jnp.where(spot, jnp.concatenate([before] * heads, axis=0), 0.0)
        high = spread.astype(BF16)
        low = (spread - high.astype(F32)).astype(BF16)
        reach = dot(dw_ref[t], jnp.concatenate([high, high], axis=0)) + dot(dw_ref[t, :, : heads * poles], low)
        for b in range(blocks):
            at = pl.ds(b * SUB, SUB)
            o_ref[at, cols] = (
                q_ref[at, cols].astype(F32) * (part_ref[at, cols] + reach[:, b * LANES : (b + 1) * LANES])
            ).astype(BF16)

    def closing(i, _):
        o = lax.rem(me + owners - i, owners) if n == owners else i

        @pl.when(o != me)
        def _():
            carry_in(o).wait_recv()

        for k in range(per_owner):
            finish(o * per_owner + k)
        result(o).start()
        return 0

    lax.fori_loop(0, owners, closing, 0)

    def drain(o, _):
        result(o).wait()

        @pl.when(o != me)
        def _():
            state_out(o).wait_send()

        @pl.when(me < n - 1)
        def _():
            halo(o).wait_send()

        return 0

    lax.fori_loop(0, owners, drain, 0)

    @pl.when(me < owners)
    def _():
        def drain_carry(e, _):
            @pl.when(e != me)
            def _():
                carry_back(e).wait_send()

            return 0

        lax.fori_loop(0, n, drain_carry, 0)


def shards(
    gate_out, gate_in, values, gate_mid, medium_taps, medium_skip, residues, rates, long_skip
):
    rows, features = gate_out.shape
    groups, poles = rates.shape
    width = features // groups
    blocks = rows // SUB
    tiles = features // LANES
    n = lax.axis_size("seq")
    owners = min(n, tiles)
    per_owner = tiles // owners
    heads = LANES // width
    stripe = (rows, features)
    vmem = pl.BlockSpec(memory_space=pltpu.VMEM)
    hbm = pl.BlockSpec(memory_space=pl.ANY)
    flops = 2 * tiles * SUB * 2 * SUB * blocks * LANES * (heads + heads // 2 + 2)
    return pl.pallas_call(
        functools.partial(kernel, n, owners, blocks, width, poles),
        out_shape=jax.ShapeDtypeStruct(stripe, BF16),
        in_specs=[hbm] * 4 + [vmem] * 5,
        out_specs=hbm,
        scratch_shapes=[
            pltpu.VMEM(stripe, BF16),
            pltpu.VMEM(stripe, BF16),
            pltpu.VMEM(stripe, BF16),
            pltpu.VMEM(stripe, BF16),
            pltpu.VMEM((rows + SUB, features), BF16),
            pltpu.VMEM(stripe, F32),
            pltpu.VMEM(stripe, BF16),
            pltpu.VMEM((tiles, heads * STRIP, 2 * SUB), BF16),
            pltpu.VMEM((tiles, heads // 2 * (STRIP + poles), 2 * SUB), BF16),
            pltpu.VMEM((tiles, SUB, 2 * heads * poles), BF16),
            pltpu.VMEM((groups, SUB), F32),
            pltpu.VMEM((tiles, poles, LANES), F32),
            pltpu.VMEM((tiles, blocks, poles, LANES), F32),
            pltpu.VMEM((tiles, poles, LANES), F32),
            pltpu.VMEM((n, per_owner, poles, LANES), F32),
            pltpu.VMEM((n, per_owner, poles, LANES), BF16),
            pltpu.VMEM((tiles, poles, LANES), BF16),
            pltpu.SemaphoreType.DMA((6,)),
            pltpu.SemaphoreType.DMA((owners,)),
            pltpu.SemaphoreType.DMA((owners,)),
            pltpu.SemaphoreType.DMA((owners,)),
            pltpu.SemaphoreType.DMA((owners,)),
            pltpu.SemaphoreType.DMA((n,)),
            pltpu.SemaphoreType.DMA((n,)),
            pltpu.SemaphoreType.DMA((owners,)),
        ],
        compiler_params=pltpu.CompilerParams(
            collective_id=0, has_side_effects=True, vmem_limit_bytes=60 * 1024 * 1024
        ),
        cost_estimate=pl.CostEstimate(flops=flops, bytes_accessed=10 * rows * features, transcendentals=0),
    )(
        gate_out,
        gate_in,
        values,
        gate_mid,
        medium_taps,
        medium_skip.reshape(1, features),
        residues.T,
        rates.T,
        long_skip.reshape(1, features),
    )


def solution(mesh):
    rows = P(("grp", "seq"), None)
    in_specs = (rows, rows, rows, rows, P(), P(), P(), P(), P())
    return jax.shard_map(shards, mesh=mesh, in_specs=in_specs, out_specs=rows, check_vma=False)
```

```python
import functools

import jax
import jax.numpy as jnp
from jax import lax
from jax.experimental import pallas as pl
from jax.experimental.pallas import tpu as pltpu
from jax.sharding import PartitionSpec as P

SUB = 128
LANES = 128
STRIP = 32
MESH = pl.DeviceIdType.MESH
F32 = jnp.float32
BF16 = jnp.bfloat16


def iota(shape, axis):
    return lax.broadcasted_iota(jnp.int32, shape, axis)


def dot(a, b):
    return jnp.dot(a, b, preferred_element_type=F32)


def toeplitz(row, shift):
    return pltpu.roll(jnp.broadcast_to(row, (STRIP, SUB)), shift, 1, stride=1, stride_axis=0)


def thirds(x):
    high = x.astype(BF16)
    rest = x - high.astype(F32)
    middle = rest.astype(BF16)
    return [high, middle, (rest - middle.astype(F32)).astype(BF16)]


def kernel(
    n,
    owners,
    blocks,
    width,
    poles,
    q_hbm,
    a_hbm,
    v_hbm,
    k_hbm,
    taps_ref,
    mskip_ref,
    res_ref,
    rates_ref,
    lskip_ref,
    out_hbm,
    q_ref,
    a_ref,
    v_ref,
    k_ref,
    ext_ref,
    part_ref,
    o_ref,
    lhsm_refs,
    lhsl_refs,
    rpm_refs,
    dw_ref,
    r0_ref,
    rp_ref,
    sp_ref,
    s0_ref,
    st_ref,
    gath_ref,
    cret_ref,
    cin_ref,
    in_sem,
    out_sem,
    halo_send,
    halo_recv,
    st_send,
    st_recv,
    c_send,
    c_recv,
):
    rows, features = q_hbm.shape
    tiles = features // LANES
    per_owner = tiles // owners
    chunk = per_owner * LANES
    heads = LANES // width
    half = heads // 2
    wide = blocks * LANES
    tail = rows - SUB
    me = lax.axis_index("seq")

    barrier = pltpu.get_barrier_semaphore()

    def greet(i, _):
        @pl.when(i != me)
        def _():
            pl.semaphore_signal(barrier, inc=1, device_id={"seq": i}, device_id_type=MESH)

        return 0

    lax.fori_loop(0, n, greet, 0)

    loads = [
        pltpu.make_async_copy(a_hbm.at[pl.ds(tail, SUB)], a_ref.at[pl.ds(tail, SUB)], in_sem.at[0]),
        pltpu.make_async_copy(v_hbm.at[pl.ds(tail, SUB)], v_ref.at[pl.ds(tail, SUB)], in_sem.at[1]),
        pltpu.make_async_copy(a_hbm.at[pl.ds(0, tail)], a_ref.at[pl.ds(0, tail)], in_sem.at[2]),
        pltpu.make_async_copy(v_hbm.at[pl.ds(0, tail)], v_ref.at[pl.ds(0, tail)], in_sem.at[3]),
        pltpu.make_async_copy(k_hbm, k_ref, in_sem.at[4]),
        pltpu.make_async_copy(q_hbm, q_ref, in_sem.at[5]),
    ]
    for load in loads:
        load.start()

    def lanes_of(t):
        return pl.ds(pl.multiple_of(t * LANES, LANES), LANES)

    def chunk_of(o):
        return pl.ds(pl.multiple_of(o * chunk, chunk), chunk)

    def multiply(start, count, cols):
        ext_ref[pl.ds(SUB + start, count), cols] = (
            a_ref[pl.ds(start, count), cols].astype(F32) * v_ref[pl.ds(start, count), cols].astype(F32)
        ).astype(BF16)

    def halo(o):
        return pltpu.make_async_remote_copy(
            src_ref=ext_ref.at[pl.ds(rows, SUB), chunk_of(o)],
            dst_ref=ext_ref.at[pl.ds(0, SUB), chunk_of(o)],
            send_sem=halo_send.at[o],
            recv_sem=halo_recv.at[o],
            device_id={"seq": jnp.minimum(me + 1, n - 1)},
            device_id_type=MESH,
        )

    loads[0].wait()
    loads[1].wait()
    pl.semaphore_wait(barrier, n - 1)

    def send_halo(i, _):
        o = lax.rem(me + 1 + i, owners)
        multiply(tail, SUB, chunk_of(o))

        @pl.when(me < n - 1)
        def _():
            halo(o).start()

        return 0

    lax.fori_loop(0, owners, send_halo, 0)

    @pl.when(me == 0)
    def _():
        ext_ref[pl.ds(0, SUB), :] = jnp.zeros((SUB, features), BF16)

    loads[2].wait()
    loads[3].wait()

    def rest(o, _):
        multiply(0, tail, chunk_of(o))
        return 0

    lax.fori_loop(0, owners, rest, 0)

    row_id = iota((SUB, SUB), 0)
    col_id = iota((SUB, SUB), 1)
    strip_row, strip_col = iota((STRIP, SUB), 0), iota((STRIP, SUB), 1)
    below = strip_col <= strip_row
    inside = strip_col <= strip_row + (SUB - STRIP)
    zero = jnp.zeros((STRIP, SUB), F32)
    mirror = (lax.rem(row_id + col_id, SUB) == 0).astype(BF16)
    r0_ref[...] = dot(taps_ref[...], mirror)
    table = jnp.concatenate(thirds(rates_ref[...]) + thirds(res_ref[...]), axis=0)
    groups = rates_ref.shape[1]
    pick_row, pick_col = iota((groups, LANES), 0), iota((groups, LANES), 1) // width

    def column(x):
        return jnp.concatenate(
            [jnp.broadcast_to(x[:, g * width : g * width + 1], (poles, LANES)) for g in range(heads)], axis=0
        )

    def weights(t, k, slot):
        lhsm_ref, lhsl_ref = lhsm_refs[slot], lhsl_refs[slot]
        spread = dot(table, (pick_row == t * heads + pick_col).astype(F32).astype(BF16))
        spread = [spread[m * poles : (m + 1) * poles] for m in range(6)]
        rp = spread[0] + spread[1] + spread[2]
        sp = spread[3] + spread[4] + spread[5]
        rp_ref[t] = rp
        sp_ref[t] = sp
        rpm_refs[slot][k] = rp
        rate_col, res_col = column(rp), column(sp)
        fold = jnp.exp(-rate_col * (SUB - 1 - col_id).astype(F32))
        weighted = (res_col * fold).reshape(heads, poles, SUB).sum(axis=1)
        line = pltpu.roll(weighted, 1, 1).astype(BF16).astype(F32)
        for r in range(half):
            first = jnp.where(inside, toeplitz(line[r : r + 1], SUB - STRIP), zero)
            second = jnp.where(inside, toeplitz(line[r + half : r + half + 1], SUB - STRIP), zero)
            lhsl_ref[k, pl.ds(r * STRIP, STRIP), :] = jnp.concatenate([first, second], axis=1).astype(BF16)
            lhsl_ref[k, pl.ds(half * STRIP + r * poles, poles), :] = jnp.concatenate(
                [fold[r * poles : (r + 1) * poles], fold[(r + half) * poles : (r + half + 1) * poles]], axis=1
            ).astype(BF16)
        for g in range(heads):
            band = toeplitz(r0_ref[pl.ds(t * heads + g, 1), :], 0)
            lhsm_ref[k, pl.ds(g * STRIP, STRIP), :] = jnp.concatenate(
                [jnp.where(below, zero, band), jnp.where(below, band, zero)], axis=1
            ).astype(BF16)

    def reach_of(t):
        rate_col, res_col = column(rp_ref[t]), column(sp_ref[t])
        reach = (res_col * jnp.exp(-rate_col * (col_id + 1).astype(F32))).T
        high = reach.astype(BF16)
        dw_ref[t] = jnp.concatenate([high, (reach - high.astype(F32)).astype(BF16)], axis=1)

    def reaches(o, _):
        for k in range(per_owner):
            reach_of(o * per_owner + k)
        return 0

    for k in range(per_owner):
        weights(lax.rem(me, owners) * per_owner + k, k, 0)
    loads[4].wait()

    strip_head = lax.rem(iota((STRIP, wide), 1), LANES) // width
    state_head = lax.rem(iota((poles, wide), 1), LANES) // width
    low = lax.rem(iota((SUB, wide), 1), LANES) // width < half

    def state_out(o):
        return pltpu.make_async_remote_copy(
            src_ref=st_ref.at[pl.ds(o * per_owner, per_owner)],
            dst_ref=gath_ref.at[me],
            send_sem=st_send.at[o],
            recv_sem=st_recv.at[me],
            device_id={"seq": o},
            device_id_type=MESH,
        )

    def side(ref, cols):
        return jnp.concatenate([ref[pl.ds(b * SUB, SUB), cols].astype(F32) for b in range(blocks)], axis=1)

    def main(t, k, slot):
        lhsm_ref, lhsl_ref = lhsm_refs[slot], lhsl_refs[slot]
        cols = lanes_of(t)
        reach = SUB + STRIP
        medium = []
        for start in range(0, SUB, STRIP):
            rhs = jnp.concatenate([ext_ref[pl.ds(b * SUB + start, reach), cols] for b in range(blocks)], axis=1)
            many = dot(lhsm_ref[k, :, :reach], rhs)
            strip = many[:STRIP]
            for g in range(1, heads):
                strip = jnp.where(strip_head == g, many[g * STRIP : (g + 1) * STRIP], strip)
            medium.append(strip)
        medium = jnp.concatenate(medium, axis=0)
        product = jnp.concatenate([ext_ref[pl.ds((b + 1) * SUB, SUB), cols] for b in range(blocks)], axis=1)
        skip = jnp.concatenate([mskip_ref[:, cols]] * blocks, axis=1)
        medium = medium + skip * product.astype(F32)
        gated = (side(k_ref, cols) * medium).astype(BF16).astype(F32)
        pad = jnp.zeros((SUB - STRIP, wide), BF16)
        first = jnp.concatenate([pad, jnp.where(low, gated, 0.0).astype(BF16)], axis=0)
        second = jnp.concatenate([pad, jnp.where(low, 0.0, gated).astype(BF16)], axis=0)
        inner = []
        for start in range(0, SUB, STRIP):
            pair = jnp.concatenate([first[start : start + SUB], second[start : start + SUB]], axis=0)
            last = start + STRIP == SUB
            many = dot(lhsl_ref[k] if last else lhsl_ref[k, : half * STRIP], pair)
            strip = many[:STRIP]
            for r in range(1, half):
                strip = jnp.where(lax.rem(strip_head, half) == r, many[r * STRIP : (r + 1) * STRIP], strip)
            inner.append(strip)
        inner = jnp.concatenate(inner, axis=0)
        base = half * STRIP
        states = many[base : base + poles]
        for r in range(1, half):
            states = jnp.where(
                lax.rem(state_head, half) == r, many[base + r * poles : base + (r + 1) * poles], states
            )
        inner = inner + jnp.concatenate([lskip_ref[:, cols]] * blocks, axis=1) * gated
        decay = jnp.exp(rpm_refs[slot][k] * (-1.0 * SUB))
        held = jnp.zeros((poles, LANES), F32)
        for b in range(blocks):
            part_ref[pl.ds(b * SUB, SUB), cols] = inner[:, b * LANES : (b + 1) * LANES]
            s0_ref[t, b] = held
            held = decay * held + states[:, b * LANES : (b + 1) * LANES]
        st_ref[t] = held

    def step(i, slot):
        o = lax.rem(me + i, owners)
        later = lax.rem(me + i + 1, owners)

        @pl.when(me > 0)
        def _():
            halo(o).wait_recv()

        for k in range(per_owner):
            main(o * per_owner + k, k, slot)
            weights(later * per_owner + k, k, 1 - slot)

        @pl.when(o != me)
        def _():
            state_out(o).start()

    def work(j, _):
        step(2 * j, 0)
        step(2 * j + 1, 1)
        return 0

    lax.fori_loop(0, owners // 2, work, 0)
    lax.fori_loop(0, owners // 2, reaches, 0)

    def carry_back(e):
        return pltpu.make_async_remote_copy(
            src_ref=cret_ref.at[e],
            dst_ref=cin_ref.at[pl.ds(me * per_owner, per_owner)],
            send_sem=c_send.at[e],
            recv_sem=c_recv.at[me],
            device_id={"seq": e},
            device_id_type=MESH,
        )

    def state_in(e):
        return pltpu.make_async_remote_copy(
            src_ref=st_ref.at[pl.ds(0, per_owner)],
            dst_ref=gath_ref.at[e],
            send_sem=st_send.at[0],
            recv_sem=st_recv.at[e],
            device_id={"seq": e},
            device_id_type=MESH,
        )

    def carry_in(o):
        return pltpu.make_async_remote_copy(
            src_ref=cret_ref.at[0],
            dst_ref=cin_ref.at[pl.ds(o * per_owner, per_owner)],
            send_sem=c_send.at[0],
            recv_sem=c_recv.at[o],
            device_id={"seq": o},
            device_id_type=MESH,
        )

    @pl.when(me < owners)
    def _():
        mine = pl.ds(me * per_owner, per_owner)
        gath_ref[me] = st_ref[mine]
        power = jnp.exp(rp_ref[mine] * (-1.0 * SUB * blocks))

        def scan(e, held):
            cret_ref[e] = held.astype(BF16)

            @pl.when(e != me)
            def _():
                state_in(e).wait_recv()

            return power * held + gath_ref[e]

        lax.fori_loop(0, n, scan, jnp.zeros((per_owner, poles, LANES), F32))

        def give(i, _):
            carry_back(lax.rem(me + i, n)).start()
            return 0

        lax.fori_loop(1, n, give, 0)
        cin_ref[mine] = cret_ref[me]

    lax.fori_loop(owners // 2, owners, reaches, 0)
    loads[5].wait()

    def result(o):
        return pltpu.make_async_copy(o_ref.at[:, chunk_of(o)], out_hbm.at[:, chunk_of(o)], out_sem.at[o])

    spot = iota((heads * poles, wide), 0) // poles == lax.rem(iota((heads * poles, wide), 1), LANES) // width

    def finish(t):
        cols = lanes_of(t)
        decay = jnp.exp(rp_ref[t] * (-1.0 * SUB))
        carried = cin_ref[t].astype(F32)
        before = []
        for b in range(blocks):
            before.append(carried + s0_ref[t, b])
            carried = decay * carried
        before = jnp.concatenate(before, axis=1)
        spread = jnp.where(spot, jnp.concatenate([before] * heads, axis=0), 0.0)
        high = spread.astype(BF16)
        low = (spread - high.astype(F32)).astype(BF16)
        reach = dot(dw_ref[t], jnp.concatenate([high, high], axis=0)) + dot(dw_ref[t, :, : heads * poles], low)
        for b in range(blocks):
            at = pl.ds(b * SUB, SUB)
            o_ref[at, cols] = (
                q_ref[at, cols].astype(F32) * (part_ref[at, cols] + reach[:, b * LANES : (b + 1) * LANES])
            ).astype(BF16)

    def closing(i, _):
        o = lax.rem(me + owners - i, owners) if n == owners else i

        @pl.when(o != me)
        def _():
            carry_in(o).wait_recv()

        for k in range(per_owner):
            finish(o * per_owner + k)
        result(o).start()
        return 0

    lax.fori_loop(0, owners, closing, 0)

    def drain(o, _):
        result(o).wait()

        @pl.when(o != me)
        def _():
            state_out(o).wait_send()

        @pl.when(me < n - 1)
        def _():
            halo(o).wait_send()

        return 0

    lax.fori_loop(0, owners, drain, 0)

    @pl.when(me < owners)
    def _():
        def drain_carry(e, _):
            @pl.when(e != me)
            def _():
                carry_back(e).wait_send()

            return 0

        lax.fori_loop(0, n, drain_carry, 0)


def shards(
    gate_out, gate_in, values, gate_mid, medium_taps, medium_skip, residues, rates, long_skip
):
    rows, features = gate_out.shape
    groups, poles = rates.shape
    width = features // groups
    blocks = rows // SUB
    tiles = features // LANES
    n = lax.axis_size("seq")
    owners = min(n, tiles)
    per_owner = tiles // owners
    heads = LANES // width
    stripe = (rows, features)
    vmem = pl.BlockSpec(memory_space=pltpu.VMEM)
    hbm = pl.BlockSpec(memory_space=pl.ANY)
    flops = 2 * tiles * SUB * 2 * SUB * blocks * LANES * (heads + heads // 2 + 2)
    return pl.pallas_call(
        functools.partial(kernel, n, owners, blocks, width, poles),
        out_shape=jax.ShapeDtypeStruct(stripe, BF16),
        in_specs=[hbm] * 4 + [vmem] * 5,
        out_specs=hbm,
        scratch_shapes=[
            pltpu.VMEM(stripe, BF16),
            pltpu.VMEM(stripe, BF16),
            pltpu.VMEM(stripe, BF16),
            pltpu.VMEM(stripe, BF16),
            pltpu.VMEM((rows + SUB, features), BF16),
            pltpu.VMEM(stripe, F32),
            pltpu.VMEM(stripe, BF16),
            [pltpu.VMEM((per_owner, heads * STRIP, 2 * SUB), BF16)] * 2,
            [pltpu.VMEM((per_owner, heads // 2 * (STRIP + poles), 2 * SUB), BF16)] * 2,
            [pltpu.VMEM((per_owner, poles, LANES), F32)] * 2,
            pltpu.VMEM((tiles, SUB, 2 * heads * poles), BF16),
            pltpu.VMEM((groups, SUB), F32),
            pltpu.VMEM((tiles, poles, LANES), F32),
            pltpu.VMEM((tiles, poles, LANES), F32),
            pltpu.VMEM((tiles, blocks, poles, LANES), F32),
            pltpu.VMEM((tiles, poles, LANES), F32),
            pltpu.VMEM((n, per_owner, poles, LANES), F32),
            pltpu.VMEM((n, per_owner, poles, LANES), BF16),
            pltpu.VMEM((tiles, poles, LANES), BF16),
            pltpu.SemaphoreType.DMA((6,)),
            pltpu.SemaphoreType.DMA((owners,)),
            pltpu.SemaphoreType.DMA((owners,)),
            pltpu.SemaphoreType.DMA((owners,)),
            pltpu.SemaphoreType.DMA((owners,)),
            pltpu.SemaphoreType.DMA((n,)),
            pltpu.SemaphoreType.DMA((n,)),
            pltpu.SemaphoreType.DMA((owners,)),
        ],
        compiler_params=pltpu.CompilerParams(
            collective_id=0, has_side_effects=True, vmem_limit_bytes=60 * 1024 * 1024
        ),
        cost_estimate=pl.CostEstimate(flops=flops, bytes_accessed=10 * rows * features, transcendentals=0),
    )(
        gate_out,
        gate_in,
        values,
        gate_mid,
        medium_taps,
        medium_skip.reshape(1, features),
        residues.T,
        rates.T,
        long_skip.reshape(1, features),
    )


def solution(mesh):
    rows = P(("grp", "seq"), None)
    in_specs = (rows, rows, rows, rows, P(), P(), P(), P(), P())
    return jax.shard_map(shards, mesh=mesh, in_specs=in_specs, out_specs=rows, check_vma=False)
```

```python
import functools

import jax
import jax.numpy as jnp
from jax import lax
from jax.experimental import pallas as pl
from jax.experimental.pallas import tpu as pltpu
from jax.sharding import PartitionSpec as P

SUB = 128
LANES = 128
STRIP = 32
MESH = pl.DeviceIdType.MESH
F32 = jnp.float32
BF16 = jnp.bfloat16


def iota(shape, axis):
    return lax.broadcasted_iota(jnp.int32, shape, axis)


def dot(a, b):
    return jnp.dot(a, b, preferred_element_type=F32)


def toeplitz(row, shift):
    return pltpu.roll(jnp.broadcast_to(row, (STRIP, SUB)), shift, 1, stride=1, stride_axis=0)


def choose(parts, index):
    bit = 1
    while len(parts) > 1:
        odd = lax.rem(index // bit, 2) == 1
        parts = [jnp.where(odd, parts[k + 1], parts[k]) for k in range(0, len(parts), 2)]
        bit *= 2
    return parts[0]


def thirds(x):
    high = x.astype(BF16)
    rest = x - high.astype(F32)
    middle = rest.astype(BF16)
    return [high, middle, (rest - middle.astype(F32)).astype(BF16)]


def kernel(
    n,
    owners,
    blocks,
    width,
    poles,
    q_hbm,
    a_hbm,
    v_hbm,
    k_hbm,
    taps_ref,
    mskip_ref,
    res_ref,
    rates_ref,
    lskip_ref,
    out_hbm,
    q_ref,
    a_ref,
    v_ref,
    k_ref,
    ext_ref,
    part_ref,
    o_ref,
    lhsm_refs,
    lhsl_refs,
    line_ref,
    fold_ref,
    dw_ref,
    r0_ref,
    rp_ref,
    sp_ref,
    s0_ref,
    st_ref,
    gath_ref,
    cret_ref,
    cin_ref,
    in_sem,
    out_sem,
    halo_send,
    halo_recv,
    st_send,
    st_recv,
    c_send,
    c_recv,
):
    rows, features = q_hbm.shape
    tiles = features // LANES
    per_owner = tiles // owners
    chunk = per_owner * LANES
    heads = LANES // width
    half = heads // 2
    wide = blocks * LANES
    tail = rows - SUB
    me = lax.axis_index("seq")

    barrier = pltpu.get_barrier_semaphore()

    def greet(i, _):
        @pl.when(i != me)
        def _():
            pl.semaphore_signal(barrier, inc=1, device_id={"seq": i}, device_id_type=MESH)

        return 0

    lax.fori_loop(0, n, greet, 0)

    loads = [
        pltpu.make_async_copy(a_hbm.at[pl.ds(tail, SUB)], a_ref.at[pl.ds(tail, SUB)], in_sem.at[0]),
        pltpu.make_async_copy(v_hbm.at[pl.ds(tail, SUB)], v_ref.at[pl.ds(tail, SUB)], in_sem.at[1]),
        pltpu.make_async_copy(a_hbm.at[pl.ds(0, tail)], a_ref.at[pl.ds(0, tail)], in_sem.at[2]),
        pltpu.make_async_copy(v_hbm.at[pl.ds(0, tail)], v_ref.at[pl.ds(0, tail)], in_sem.at[3]),
        pltpu.make_async_copy(k_hbm, k_ref, in_sem.at[4]),
        pltpu.make_async_copy(q_hbm, q_ref, in_sem.at[5]),
    ]
    for load in loads:
        load.start()

    def lanes_of(t):
        return pl.ds(pl.multiple_of(t * LANES, LANES), LANES)

    def chunk_of(o):
        return pl.ds(pl.multiple_of(o * chunk, chunk), chunk)

    def multiply(start, count, cols):
        ext_ref[pl.ds(SUB + start, count), cols] = (
            a_ref[pl.ds(start, count), cols].astype(F32) * v_ref[pl.ds(start, count), cols].astype(F32)
        ).astype(BF16)

    def halo(o):
        return pltpu.make_async_remote_copy(
            src_ref=ext_ref.at[pl.ds(rows, SUB), chunk_of(o)],
            dst_ref=ext_ref.at[pl.ds(0, SUB), chunk_of(o)],
            send_sem=halo_send.at[o],
            recv_sem=halo_recv.at[o],
            device_id={"seq": jnp.minimum(me + 1, n - 1)},
            device_id_type=MESH,
        )

    loads[0].wait()
    loads[1].wait()
    pl.semaphore_wait(barrier, n - 1)

    def send_halo(i, _):
        o = lax.rem(me + 1 + i, owners)
        multiply(tail, SUB, chunk_of(o))

        @pl.when(me < n - 1)
        def _():
            halo(o).start()

        return 0

    lax.fori_loop(0, owners, send_halo, 0)

    @pl.when(me == 0)
    def _():
        ext_ref[pl.ds(0, SUB), :] = jnp.zeros((SUB, features), BF16)

    loads[2].wait()
    loads[3].wait()

    def rest(o, _):
        multiply(0, tail, chunk_of(o))
        return 0

    lax.fori_loop(0, owners, rest, 0)

    row_id = iota((SUB, SUB), 0)
    col_id = iota((SUB, SUB), 1)
    strip_row, strip_col = iota((STRIP, SUB), 0), iota((STRIP, SUB), 1)
    below = strip_col <= strip_row
    inside = strip_col <= strip_row + (SUB - STRIP)
    zero = jnp.zeros((STRIP, SUB), F32)
    mirror = (lax.rem(row_id + col_id, SUB) == 0).astype(BF16)
    r0_ref[...] = dot(taps_ref[...], mirror)
    table = jnp.concatenate(thirds(rates_ref[...]) + thirds(res_ref[...]), axis=0)
    groups = rates_ref.shape[1]
    pick_row, pick_col = iota((groups, LANES), 0), iota((groups, LANES), 1) // width

    def column(x):
        return jnp.concatenate(
            [jnp.broadcast_to(x[:, g * width : g * width + 1], (poles, LANES)) for g in range(heads)], axis=0
        )

    def tables(t):
        spread = dot(table, (pick_row == t * heads + pick_col).astype(F32).astype(BF16))
        spread = [spread[m * poles : (m + 1) * poles] for m in range(6)]
        rp = spread[0] + spread[1] + spread[2]
        sp = spread[3] + spread[4] + spread[5]
        rp_ref[t] = rp
        sp_ref[t] = sp
        rate_col, res_col = column(rp), column(sp)
        fold = jnp.exp(-rate_col * (SUB - 1 - col_id).astype(F32))
        weighted = (res_col * fold).reshape(heads, poles, SUB).sum(axis=1)
        line_ref[t] = pltpu.roll(weighted, 1, 1).astype(BF16).astype(F32)
        middle = half * poles
        fold_ref[t] = jnp.concatenate([fold[:middle], fold[middle:]], axis=1).astype(BF16)

    def tables_of(o, _):
        for k in range(per_owner):
            tables(o * per_owner + k)
        return 0

    lax.fori_loop(0, owners, tables_of, 0)

    def weights(t, k, slot):
        lhsm_ref, lhsl_ref = lhsm_refs[slot], lhsl_refs[slot]
        line = line_ref[t]
        lhsl_ref[k, pl.ds(half * STRIP, half * poles), :] = fold_ref[t]
        for r in range(half):
            first = jnp.where(inside, toeplitz(line[r : r + 1], SUB - STRIP), zero)
            second = jnp.where(inside, toeplitz(line[r + half : r + half + 1], SUB - STRIP), zero)
            lhsl_ref[k, pl.ds(r * STRIP, STRIP), :] = jnp.concatenate([first, second], axis=1).astype(BF16)
        for g in range(heads):
            band = toeplitz(r0_ref[pl.ds(t * heads + g, 1), :], 0)
            lhsm_ref[k, pl.ds(g * STRIP, STRIP), :] = jnp.concatenate(
                [jnp.where(below, zero, band), jnp.where(below, band, zero)], axis=1
            ).astype(BF16)

    def reach_of(t):
        rate_col, res_col = column(rp_ref[t]), column(sp_ref[t])
        reach = (res_col * jnp.exp(-rate_col * (col_id + 1).astype(F32))).T
        high = reach.astype(BF16)
        dw_ref[t] = jnp.concatenate([high, (reach - high.astype(F32)).astype(BF16)], axis=1)

    def reaches(o, _):
        for k in range(per_owner):
            reach_of(o * per_owner + k)
        return 0

    for k in range(per_owner):
        weights(lax.rem(me, owners) * per_owner + k, k, 0)
    loads[4].wait()

    lane_head = iota((8, LANES), 1) // width
    lane_head = jnp.concatenate([lane_head] * blocks, axis=1)
    strip_head = jnp.concatenate([lane_head] * (STRIP // 8), axis=0)
    state_head = jnp.concatenate([lane_head] * (poles // 8), axis=0)
    low = jnp.concatenate([lane_head] * (SUB // 8), axis=0) < half

    def state_out(o):
        return pltpu.make_async_remote_copy(
            src_ref=st_ref.at[pl.ds(o * per_owner, per_owner)],
            dst_ref=gath_ref.at[me],
            send_sem=st_send.at[o],
            recv_sem=st_recv.at[me],
            device_id={"seq": o},
            device_id_type=MESH,
        )

    def side(ref, cols):
        return jnp.concatenate([ref[pl.ds(b * SUB, SUB), cols].astype(F32) for b in range(blocks)], axis=1)

    def main(t, k, slot):
        lhsm_ref, lhsl_ref = lhsm_refs[slot], lhsl_refs[slot]
        cols = lanes_of(t)
        reach = SUB + STRIP
        medium = []
        for start in range(0, SUB, STRIP):
            rhs = jnp.concatenate([ext_ref[pl.ds(b * SUB + start, reach), cols] for b in range(blocks)], axis=1)
            many = dot(lhsm_ref[k, :, :reach], rhs)
            medium.append(choose([many[g * STRIP : (g + 1) * STRIP] for g in range(heads)], strip_head))
        medium = jnp.concatenate(medium, axis=0)
        product = jnp.concatenate([ext_ref[pl.ds((b + 1) * SUB, SUB), cols] for b in range(blocks)], axis=1)
        skip = jnp.concatenate([mskip_ref[:, cols]] * blocks, axis=1)
        medium = medium + skip * product.astype(F32)
        gated = (side(k_ref, cols) * medium).astype(BF16).astype(F32)
        pad = jnp.zeros((SUB - STRIP, wide), BF16)
        first = jnp.concatenate([pad, jnp.where(low, gated, 0.0).astype(BF16)], axis=0)
        second = jnp.concatenate([pad, jnp.where(low, 0.0, gated).astype(BF16)], axis=0)
        inner = []
        for start in range(0, SUB, STRIP):
            pair = jnp.concatenate([first[start : start + SUB], second[start : start + SUB]], axis=0)
            last = start + STRIP == SUB
            many = dot(lhsl_ref[k] if last else lhsl_ref[k, : half * STRIP], pair)
            inner.append(choose([many[r * STRIP : (r + 1) * STRIP] for r in range(half)], strip_head))
        inner = jnp.concatenate(inner, axis=0)
        base = half * STRIP
        states = choose([many[base + r * poles : base + (r + 1) * poles] for r in range(half)], state_head)
        inner = inner + jnp.concatenate([lskip_ref[:, cols]] * blocks, axis=1) * gated
        decay = jnp.exp(rp_ref[t] * (-1.0 * SUB))
        held = jnp.zeros((poles, LANES), F32)
        for b in range(blocks):
            part_ref[pl.ds(b * SUB, SUB), cols] = inner[:, b * LANES : (b + 1) * LANES]
            s0_ref[t, b] = held
            held = decay * held + states[:, b * LANES : (b + 1) * LANES]
        st_ref[t] = held

    def step(i, slot):
        o = lax.rem(me + i, owners)
        later = lax.rem(me + i + 1, owners)

        @pl.when(me > 0)
        def _():
            halo(o).wait_recv()

        for k in range(per_owner):
            main(o * per_owner + k, k, slot)
            weights(later * per_owner + k, k, 1 - slot)

        @pl.when(o != me)
        def _():
            state_out(o).start()

    def work(j, _):
        step(2 * j, 0)
        step(2 * j + 1, 1)
        return 0

    lax.fori_loop(0, owners // 2, work, 0)
    lax.fori_loop(0, owners // 2, reaches, 0)

    def carry_back(e):
        return pltpu.make_async_remote_copy(
            src_ref=cret_ref.at[e],
            dst_ref=cin_ref.at[pl.ds(me * per_owner, per_owner)],
            send_sem=c_send.at[e],
            recv_sem=c_recv.at[me],
            device_id={"seq": e},
            device_id_type=MESH,
        )

    def state_in(e):
        return pltpu.make_async_remote_copy(
            src_ref=st_ref.at[pl.ds(0, per_owner)],
            dst_ref=gath_ref.at[e],
            send_sem=st_send.at[0],
            recv_sem=st_recv.at[e],
            device_id={"seq": e},
            device_id_type=MESH,
        )

    def carry_in(o):
        return pltpu.make_async_remote_copy(
            src_ref=cret_ref.at[0],
            dst_ref=cin_ref.at[pl.ds(o * per_owner, per_owner)],
            send_sem=c_send.at[0],
            recv_sem=c_recv.at[o],
            device_id={"seq": o},
            device_id_type=MESH,
        )

    @pl.when(me < owners)
    def _():
        mine = pl.ds(me * per_owner, per_owner)
        gath_ref[me] = st_ref[mine]
        power = jnp.exp(rp_ref[mine] * (-1.0 * SUB * blocks))

        def scan(e, held):
            cret_ref[e] = held.astype(BF16)

            @pl.when(e != me)
            def _():
                state_in(e).wait_recv()

            return power * held + gath_ref[e]

        lax.fori_loop(0, n, scan, jnp.zeros((per_owner, poles, LANES), F32))

        def give(i, _):
            carry_back(lax.rem(me + i, n)).start()
            return 0

        lax.fori_loop(1, n, give, 0)
        cin_ref[mine] = cret_ref[me]

    lax.fori_loop(owners // 2, owners, reaches, 0)
    loads[5].wait()

    def result(o):
        return pltpu.make_async_copy(o_ref.at[:, chunk_of(o)], out_hbm.at[:, chunk_of(o)], out_sem.at[o])

    spot = iota((heads * poles, wide), 0) // poles == lax.rem(iota((heads * poles, wide), 1), LANES) // width

    def finish(t):
        cols = lanes_of(t)
        decay = jnp.exp(rp_ref[t] * (-1.0 * SUB))
        carried = cin_ref[t].astype(F32)
        before = []
        for b in range(blocks):
            before.append(carried + s0_ref[t, b])
            carried = decay * carried
        before = jnp.concatenate(before, axis=1)
        spread = jnp.where(spot, jnp.concatenate([before] * heads, axis=0), 0.0)
        high = spread.astype(BF16)
        low = (spread - high.astype(F32)).astype(BF16)
        reach = dot(dw_ref[t], jnp.concatenate([high, high], axis=0)) + dot(dw_ref[t, :, : heads * poles], low)
        for b in range(blocks):
            at = pl.ds(b * SUB, SUB)
            o_ref[at, cols] = (
                q_ref[at, cols].astype(F32) * (part_ref[at, cols] + reach[:, b * LANES : (b + 1) * LANES])
            ).astype(BF16)

    def closing(i, _):
        o = lax.rem(me + owners - i, owners) if n == owners else i

        @pl.when(o != me)
        def _():
            carry_in(o).wait_recv()

        for k in range(per_owner):
            finish(o * per_owner + k)
        result(o).start()
        return 0

    lax.fori_loop(0, owners, closing, 0)

    def drain(o, _):
        result(o).wait()

        @pl.when(o != me)
        def _():
            state_out(o).wait_send()

        @pl.when(me < n - 1)
        def _():
            halo(o).wait_send()

        return 0

    lax.fori_loop(0, owners, drain, 0)

    @pl.when(me < owners)
    def _():
        def drain_carry(e, _):
            @pl.when(e != me)
            def _():
                carry_back(e).wait_send()

            return 0

        lax.fori_loop(0, n, drain_carry, 0)


def shards(
    gate_out, gate_in, values, gate_mid, medium_taps, medium_skip, residues, rates, long_skip
):
    rows, features = gate_out.shape
    groups, poles = rates.shape
    width = features // groups
    blocks = rows // SUB
    tiles = features // LANES
    n = lax.axis_size("seq")
    owners = min(n, tiles)
    per_owner = tiles // owners
    heads = LANES // width
    stripe = (rows, features)
    vmem = pl.BlockSpec(memory_space=pltpu.VMEM)
    hbm = pl.BlockSpec(memory_space=pl.ANY)
    flops = 2 * tiles * SUB * 2 * SUB * blocks * LANES * (heads + heads // 2 + 2)
    return pl.pallas_call(
        functools.partial(kernel, n, owners, blocks, width, poles),
        out_shape=jax.ShapeDtypeStruct(stripe, BF16),
        in_specs=[hbm] * 4 + [vmem] * 5,
        out_specs=hbm,
        scratch_shapes=[
            pltpu.VMEM(stripe, BF16),
            pltpu.VMEM(stripe, BF16),
            pltpu.VMEM(stripe, BF16),
            pltpu.VMEM(stripe, BF16),
            pltpu.VMEM((rows + SUB, features), BF16),
            pltpu.VMEM(stripe, F32),
            pltpu.VMEM(stripe, BF16),
            [pltpu.VMEM((per_owner, heads * STRIP, 2 * SUB), BF16)] * 2,
            [pltpu.VMEM((per_owner, heads // 2 * (STRIP + poles), 2 * SUB), BF16)] * 2,
            pltpu.VMEM((tiles, heads, SUB), F32),
            pltpu.VMEM((tiles, heads // 2 * poles, 2 * SUB), BF16),
            pltpu.VMEM((tiles, SUB, 2 * heads * poles), BF16),
            pltpu.VMEM((groups, SUB), F32),
            pltpu.VMEM((tiles, poles, LANES), F32),
            pltpu.VMEM((tiles, poles, LANES), F32),
            pltpu.VMEM((tiles, blocks, poles, LANES), F32),
            pltpu.VMEM((tiles, poles, LANES), F32),
            pltpu.VMEM((n, per_owner, poles, LANES), F32),
            pltpu.VMEM((n, per_owner, poles, LANES), BF16),
            pltpu.VMEM((tiles, poles, LANES), BF16),
            pltpu.SemaphoreType.DMA((6,)),
            pltpu.SemaphoreType.DMA((owners,)),
            pltpu.SemaphoreType.DMA((owners,)),
            pltpu.SemaphoreType.DMA((owners,)),
            pltpu.SemaphoreType.DMA((owners,)),
            pltpu.SemaphoreType.DMA((n,)),
            pltpu.SemaphoreType.DMA((n,)),
            pltpu.SemaphoreType.DMA((owners,)),
        ],
        compiler_params=pltpu.CompilerParams(
            collective_id=0, has_side_effects=True, vmem_limit_bytes=60 * 1024 * 1024
        ),
        cost_estimate=pl.CostEstimate(flops=flops, bytes_accessed=10 * rows * features, transcendentals=0),
    )(
        gate_out,
        gate_in,
        values,
        gate_mid,
        medium_taps,
        medium_skip.reshape(1, features),
        residues.T,
        rates.T,
        long_skip.reshape(1, features),
    )


def solution(mesh):
    rows = P(("grp", "seq"), None)
    in_specs = (rows, rows, rows, rows, P(), P(), P(), P(), P())
    return jax.shard_map(shards, mesh=mesh, in_specs=in_specs, out_specs=rows, check_vma=False)
```

```python
import functools
import math

import jax
import jax.numpy as jnp
from jax import lax
from jax.experimental import pallas as pl
from jax.experimental.pallas import tpu as pltpu
from jax.sharding import PartitionSpec as P

SUB = 128
LANES = 128
STRIP = 32
MESH = pl.DeviceIdType.MESH
F32 = jnp.float32
BF16 = jnp.bfloat16


def iota(shape, axis):
    return lax.broadcasted_iota(jnp.int32, shape, axis)


def dot(a, b):
    return jnp.dot(a, b, preferred_element_type=F32)


def toeplitz(row, shift):
    return pltpu.roll(jnp.broadcast_to(row, (STRIP, SUB)), shift, 1, stride=1, stride_axis=0)


def choose(parts, index):
    bit = 1
    while len(parts) > 1:
        odd = lax.rem(index // bit, 2) == 1
        parts = [jnp.where(odd, parts[k + 1], parts[k]) for k in range(0, len(parts), 2)]
        bit *= 2
    return parts[0]


def thirds(x):
    high = x.astype(BF16)
    rest = x - high.astype(F32)
    middle = rest.astype(BF16)
    return [high, middle, (rest - middle.astype(F32)).astype(BF16)]


def kernel(
    n,
    owners,
    blocks,
    width,
    poles,
    a_hbm,
    v_hbm,
    k_hbm,
    taps_ref,
    mskip_ref,
    res_ref,
    rates_ref,
    lskip_ref,
    part_hbm,
    dw_hbm,
    before_hbm,
    a_ref,
    v_ref,
    k_ref,
    ext_ref,
    part_ref,
    lhsm_refs,
    lhsl_refs,
    line_ref,
    fold_ref,
    dw_ref,
    r0_ref,
    rp_ref,
    sp_ref,
    s0_ref,
    before_ref,
    st_ref,
    gath_ref,
    cret_ref,
    cin_ref,
    in_sem,
    out_sem,
    dw_sem,
    halo_send,
    halo_recv,
    st_send,
    st_recv,
    c_send,
    c_recv,
):
    rows, features = a_hbm.shape
    tiles = features // LANES
    per_owner = tiles // owners
    chunk = per_owner * LANES
    heads = LANES // width
    half = heads // 2
    wide = blocks * LANES
    tail = rows - SUB
    me = lax.axis_index("seq")

    barrier = pltpu.get_barrier_semaphore()

    def greet(i, _):
        @pl.when(i != me)
        def _():
            pl.semaphore_signal(barrier, inc=1, device_id={"seq": i}, device_id_type=MESH)

        return 0

    lax.fori_loop(0, n, greet, 0)

    loads = [
        pltpu.make_async_copy(a_hbm.at[pl.ds(tail, SUB)], a_ref.at[pl.ds(tail, SUB)], in_sem.at[0]),
        pltpu.make_async_copy(v_hbm.at[pl.ds(tail, SUB)], v_ref.at[pl.ds(tail, SUB)], in_sem.at[1]),
        pltpu.make_async_copy(a_hbm.at[pl.ds(0, tail)], a_ref.at[pl.ds(0, tail)], in_sem.at[2]),
        pltpu.make_async_copy(v_hbm.at[pl.ds(0, tail)], v_ref.at[pl.ds(0, tail)], in_sem.at[3]),
        pltpu.make_async_copy(k_hbm, k_ref, in_sem.at[4]),
    ]
    for load in loads:
        load.start()

    def lanes_of(t):
        return pl.ds(pl.multiple_of(t * LANES, LANES), LANES)

    def chunk_of(o):
        return pl.ds(pl.multiple_of(o * chunk, chunk), chunk)

    def multiply(start, count, cols):
        ext_ref[pl.ds(SUB + start, count), cols] = (
            a_ref[pl.ds(start, count), cols].astype(F32) * v_ref[pl.ds(start, count), cols].astype(F32)
        ).astype(BF16)

    def halo(o):
        return pltpu.make_async_remote_copy(
            src_ref=ext_ref.at[pl.ds(rows, SUB), chunk_of(o)],
            dst_ref=ext_ref.at[pl.ds(0, SUB), chunk_of(o)],
            send_sem=halo_send.at[o],
            recv_sem=halo_recv.at[o],
            device_id={"seq": jnp.minimum(me + 1, n - 1)},
            device_id_type=MESH,
        )

    loads[0].wait()
    loads[1].wait()
    pl.semaphore_wait(barrier, n - 1)

    def send_halo(i, _):
        o = lax.rem(me + 1 + i, owners)
        multiply(tail, SUB, chunk_of(o))

        @pl.when(me < n - 1)
        def _():
            halo(o).start()

        return 0

    lax.fori_loop(0, owners, send_halo, 0)

    @pl.when(me == 0)
    def _():
        ext_ref[pl.ds(0, SUB), :] = jnp.zeros((SUB, features), BF16)

    loads[2].wait()
    loads[3].wait()

    def rest(o, _):
        multiply(0, tail, chunk_of(o))
        return 0

    lax.fori_loop(0, owners, rest, 0)

    row_id = iota((SUB, SUB), 0)
    col_id = iota((SUB, SUB), 1)
    strip_row, strip_col = iota((STRIP, SUB), 0), iota((STRIP, SUB), 1)
    below = strip_col <= strip_row
    inside = strip_col <= strip_row + (SUB - STRIP)
    zero = jnp.zeros((STRIP, SUB), F32)
    mirror = (lax.rem(row_id + col_id, SUB) == 0).astype(BF16)
    r0_ref[...] = dot(taps_ref[...], mirror)
    table = jnp.concatenate(thirds(rates_ref[...]) + thirds(res_ref[...]), axis=0)
    groups = rates_ref.shape[1]
    pick_row, pick_col = iota((groups, LANES), 0), iota((groups, LANES), 1) // width

    def column(x):
        return jnp.concatenate(
            [jnp.broadcast_to(x[:, g * width : g * width + 1], (poles, LANES)) for g in range(heads)], axis=0
        )

    def tables(t):
        spread = dot(table, (pick_row == t * heads + pick_col).astype(F32).astype(BF16))
        spread = [spread[m * poles : (m + 1) * poles] for m in range(6)]
        rp = spread[0] + spread[1] + spread[2]
        sp = spread[3] + spread[4] + spread[5]
        rp_ref[t] = rp
        sp_ref[t] = sp
        rate_col, res_col = column(rp), column(sp)
        fold = jnp.exp(-rate_col * (SUB - 1 - col_id).astype(F32))
        weighted = (res_col * fold).reshape(heads, poles, SUB).sum(axis=1)
        line_ref[t] = pltpu.roll(weighted, 1, 1).astype(BF16).astype(F32)
        middle = half * poles
        fold_ref[t] = jnp.concatenate([fold[:middle], fold[middle:]], axis=1).astype(BF16)

    def tables_of(o, _):
        for k in range(per_owner):
            tables(o * per_owner + k)
        return 0

    lax.fori_loop(0, owners, tables_of, 0)

    def weights(t, k, slot):
        lhsm_ref, lhsl_ref = lhsm_refs[slot], lhsl_refs[slot]
        line = line_ref[t]
        lhsl_ref[k, pl.ds(half * STRIP, half * poles), :] = fold_ref[t]
        for r in range(half):
            first = jnp.where(inside, toeplitz(line[r : r + 1], SUB - STRIP), zero)
            second = jnp.where(inside, toeplitz(line[r + half : r + half + 1], SUB - STRIP), zero)
            lhsl_ref[k, pl.ds(r * STRIP, STRIP), :] = jnp.concatenate([first, second], axis=1).astype(BF16)
        for g in range(heads):
            band = toeplitz(r0_ref[pl.ds(t * heads + g, 1), :], 0)
            lhsm_ref[k, pl.ds(g * STRIP, STRIP), :] = jnp.concatenate(
                [jnp.where(below, zero, band), jnp.where(below, band, zero)], axis=1
            ).astype(BF16)

    def reach_of(t):
        rate_col, res_col = column(rp_ref[t]), column(sp_ref[t])
        reach = (res_col * jnp.exp(-rate_col * (col_id + 1).astype(F32))).T
        high = reach.astype(BF16)
        dw_ref[t] = jnp.concatenate([high, (reach - high.astype(F32)).astype(BF16)], axis=1)

    def reaches(o, _):
        for k in range(per_owner):
            reach_of(o * per_owner + k)
        return 0

    for k in range(per_owner):
        weights(lax.rem(me, owners) * per_owner + k, k, 0)
    loads[4].wait()

    lane_head = iota((8, LANES), 1) // width
    lane_head = jnp.concatenate([lane_head] * blocks, axis=1)
    strip_head = jnp.concatenate([lane_head] * (STRIP // 8), axis=0)
    state_head = jnp.concatenate([lane_head] * (poles // 8), axis=0)
    low = jnp.concatenate([lane_head] * (SUB // 8), axis=0) < half

    def state_out(o):
        return pltpu.make_async_remote_copy(
            src_ref=st_ref.at[pl.ds(o * per_owner, per_owner)],
            dst_ref=gath_ref.at[me],
            send_sem=st_send.at[o],
            recv_sem=st_recv.at[me],
            device_id={"seq": o},
            device_id_type=MESH,
        )

    def side(ref, cols):
        return jnp.concatenate([ref[pl.ds(b * SUB, SUB), cols].astype(F32) for b in range(blocks)], axis=1)

    def main(t, k, slot):
        lhsm_ref, lhsl_ref = lhsm_refs[slot], lhsl_refs[slot]
        cols = lanes_of(t)
        reach = SUB + STRIP
        medium = []
        for start in range(0, SUB, STRIP):
            rhs = jnp.concatenate([ext_ref[pl.ds(b * SUB + start, reach), cols] for b in range(blocks)], axis=1)
            many = dot(lhsm_ref[k, :, :reach], rhs)
            medium.append(choose([many[g * STRIP : (g + 1) * STRIP] for g in range(heads)], strip_head))
        medium = jnp.concatenate(medium, axis=0)
        product = jnp.concatenate([ext_ref[pl.ds((b + 1) * SUB, SUB), cols] for b in range(blocks)], axis=1)
        skip = jnp.concatenate([mskip_ref[:, cols]] * blocks, axis=1)
        medium = medium + skip * product.astype(F32)
        gated = (side(k_ref, cols) * medium).astype(BF16).astype(F32)
        pad = jnp.zeros((SUB - STRIP, wide), BF16)
        first = jnp.concatenate([pad, jnp.where(low, gated, 0.0).astype(BF16)], axis=0)
        second = jnp.concatenate([pad, jnp.where(low, 0.0, gated).astype(BF16)], axis=0)
        inner = []
        for start in range(0, SUB, STRIP):
            pair = jnp.concatenate([first[start : start + SUB], second[start : start + SUB]], axis=0)
            last = start + STRIP == SUB
            many = dot(lhsl_ref[k] if last else lhsl_ref[k, : half * STRIP], pair)
            inner.append(choose([many[r * STRIP : (r + 1) * STRIP] for r in range(half)], strip_head))
        inner = jnp.concatenate(inner, axis=0)
        base = half * STRIP
        states = choose([many[base + r * poles : base + (r + 1) * poles] for r in range(half)], state_head)
        inner = inner + jnp.concatenate([lskip_ref[:, cols]] * blocks, axis=1) * gated
        decay = jnp.exp(rp_ref[t] * (-1.0 * SUB))
        held = jnp.zeros((poles, LANES), F32)
        for b in range(blocks):
            part_ref[pl.ds(b * SUB, SUB), cols] = inner[:, b * LANES : (b + 1) * LANES]
            s0_ref[t, b] = held
            held = decay * held + states[:, b * LANES : (b + 1) * LANES]
        st_ref[t] = held.astype(BF16)

    def result(o):
        return pltpu.make_async_copy(part_ref.at[:, chunk_of(o)], part_hbm.at[:, chunk_of(o)], out_sem.at[o])

    def step(i, slot):
        o = lax.rem(me + i, owners)
        later = lax.rem(me + i + 1, owners)

        @pl.when(me > 0)
        def _():
            halo(o).wait_recv()

        for k in range(per_owner):
            main(o * per_owner + k, k, slot)
            weights(later * per_owner + k, k, 1 - slot)
        result(o).start()

        @pl.when(o != me)
        def _():
            state_out(o).start()

    def work(j, _):
        step(2 * j, 0)
        step(2 * j + 1, 1)
        return 0

    lax.fori_loop(0, owners // 2, work, 0)
    middle = tiles // 2

    def reach_out(k):
        at = pl.ds(k * middle, middle)
        return pltpu.make_async_copy(dw_ref.at[at], dw_hbm.at[at], dw_sem.at[k])

    lax.fori_loop(0, owners // 2, reaches, 0)
    reach_out(0).start()

    def carry_back(e):
        return pltpu.make_async_remote_copy(
            src_ref=cret_ref.at[e],
            dst_ref=cin_ref.at[pl.ds(me * per_owner, per_owner)],
            send_sem=c_send.at[e],
            recv_sem=c_recv.at[me],
            device_id={"seq": e},
            device_id_type=MESH,
        )

    def state_in(e):
        return pltpu.make_async_remote_copy(
            src_ref=st_ref.at[pl.ds(0, per_owner)],
            dst_ref=gath_ref.at[e],
            send_sem=st_send.at[0],
            recv_sem=st_recv.at[e],
            device_id={"seq": e},
            device_id_type=MESH,
        )

    def carry_in(o):
        return pltpu.make_async_remote_copy(
            src_ref=cret_ref.at[0],
            dst_ref=cin_ref.at[pl.ds(o * per_owner, per_owner)],
            send_sem=c_send.at[0],
            recv_sem=c_recv.at[o],
            device_id={"seq": o},
            device_id_type=MESH,
        )

    @pl.when(me < owners)
    def _():
        mine = pl.ds(me * per_owner, per_owner)
        gath_ref[me] = st_ref[mine]
        power = jnp.exp(rp_ref[mine] * (-1.0 * SUB * blocks))

        def scan(e, held):
            cret_ref[e] = held.astype(BF16)

            @pl.when(e != me)
            def _():
                state_in(e).wait_recv()

            return power * held + gath_ref[e].astype(F32)

        lax.fori_loop(0, n, scan, jnp.zeros((per_owner, poles, LANES), F32))

        def give(i, _):
            carry_back(lax.rem(me + i, n)).start()
            return 0

        lax.fori_loop(1, n, give, 0)
        cin_ref[mine] = cret_ref[me]

    lax.fori_loop(owners // 2, owners, reaches, 0)
    reach_out(1).start()

    def closing(i, _):
        o = lax.rem(me + owners - i, owners) if n == owners else i

        @pl.when(o != me)
        def _():
            carry_in(o).wait_recv()

        for k in range(per_owner):
            t = o * per_owner + k
            decay = jnp.exp(rp_ref[t] * (-1.0 * SUB))
            carried = cin_ref[t].astype(F32)
            for b in range(blocks):
                before_ref[t, :, pl.ds(b * LANES, LANES)] = carried + s0_ref[t, b]
                carried = decay * carried
        return 0

    lax.fori_loop(0, owners, closing, 0)
    finals = pltpu.make_async_copy(before_ref, before_hbm, dw_sem.at[2])
    finals.start()

    def drain(o, _):
        result(o).wait()

        @pl.when(o != me)
        def _():
            state_out(o).wait_send()

        @pl.when(me < n - 1)
        def _():
            halo(o).wait_send()

        return 0

    lax.fori_loop(0, owners, drain, 0)
    for copy in (reach_out(0), reach_out(1), finals):
        copy.wait()

    @pl.when(me < owners)
    def _():
        def drain_carry(e, _):
            @pl.when(e != me)
            def _():
                carry_back(e).wait_send()

            return 0

        lax.fori_loop(0, n, drain_carry, 0)


def finish(poles, width, q_ref, part_ref, dw_ref, before_ref, out_ref):
    count, _, wide = before_ref.shape
    heads = LANES // width
    shape = (heads * poles, LANES)
    spot = iota(shape, 0) // poles == iota(shape, 1) // width
    for t in range(count):
        cols = pl.ds(t * LANES, LANES)
        for b in range(wide // LANES):
            at = pl.ds(b * SUB, SUB)
            before = before_ref[t, :, pl.ds(b * LANES, LANES)]
            spread = jnp.where(spot, jnp.concatenate([before] * heads, axis=0), 0.0)
            high = spread.astype(BF16)
            low = (spread - high.astype(F32)).astype(BF16)
            reach = dot(dw_ref[t], jnp.concatenate([high, high], axis=0)) + dot(dw_ref[t, :, : heads * poles], low)
            out_ref[at, cols] = (q_ref[at, cols].astype(F32) * (part_ref[at, cols] + reach)).astype(BF16)


def shards(
    gate_out, gate_in, values, gate_mid, medium_taps, medium_skip, residues, rates, long_skip
):
    rows, features = gate_out.shape
    groups, poles = rates.shape
    width = features // groups
    blocks = rows // SUB
    tiles = features // LANES
    n = lax.axis_size("seq")
    owners = min(n, tiles)
    per_owner = tiles // owners
    heads = LANES // width
    stripe = (rows, features)
    vmem = pl.BlockSpec(memory_space=pltpu.VMEM)
    hbm = pl.BlockSpec(memory_space=pl.ANY)
    flops = 2 * tiles * SUB * 2 * SUB * blocks * LANES * (heads + heads // 2 + 2)
    part, dw, before = pl.pallas_call(
        functools.partial(kernel, n, owners, blocks, width, poles),
        out_shape=[
            jax.ShapeDtypeStruct(stripe, F32),
            jax.ShapeDtypeStruct((tiles, SUB, 2 * heads * poles), BF16),
            jax.ShapeDtypeStruct((tiles, poles, blocks * LANES), F32),
        ],
        in_specs=[hbm] * 3 + [vmem] * 5,
        out_specs=[hbm] * 3,
        scratch_shapes=[
            pltpu.VMEM(stripe, BF16),
            pltpu.VMEM(stripe, BF16),
            pltpu.VMEM(stripe, BF16),
            pltpu.VMEM((rows + SUB, features), BF16),
            pltpu.VMEM(stripe, F32),
            [pltpu.VMEM((per_owner, heads * STRIP, 2 * SUB), BF16)] * 2,
            [pltpu.VMEM((per_owner, heads // 2 * (STRIP + poles), 2 * SUB), BF16)] * 2,
            pltpu.VMEM((tiles, heads, SUB), F32),
            pltpu.VMEM((tiles, heads // 2 * poles, 2 * SUB), BF16),
            pltpu.VMEM((tiles, SUB, 2 * heads * poles), BF16),
            pltpu.VMEM((groups, SUB), F32),
            pltpu.VMEM((tiles, poles, LANES), F32),
            pltpu.VMEM((tiles, poles, LANES), F32),
            pltpu.VMEM((tiles, blocks, poles, LANES), F32),
            pltpu.VMEM((tiles, poles, blocks * LANES), F32),
            pltpu.VMEM((tiles, poles, LANES), BF16),
            pltpu.VMEM((n, per_owner, poles, LANES), BF16),
            pltpu.VMEM((n, per_owner, poles, LANES), BF16),
            pltpu.VMEM((tiles, poles, LANES), BF16),
            pltpu.SemaphoreType.DMA((5,)),
            pltpu.SemaphoreType.DMA((owners,)),
            pltpu.SemaphoreType.DMA((3,)),
            pltpu.SemaphoreType.DMA((owners,)),
            pltpu.SemaphoreType.DMA((owners,)),
            pltpu.SemaphoreType.DMA((owners,)),
            pltpu.SemaphoreType.DMA((n,)),
            pltpu.SemaphoreType.DMA((n,)),
            pltpu.SemaphoreType.DMA((owners,)),
        ],
        compiler_params=pltpu.CompilerParams(
            collective_id=0, has_side_effects=True, vmem_limit_bytes=60 * 1024 * 1024
        ),
        cost_estimate=pl.CostEstimate(flops=flops, bytes_accessed=10 * rows * features, transcendentals=0),
    )(
        gate_in,
        values,
        gate_mid,
        medium_taps,
        medium_skip.reshape(1, features),
        residues.T,
        rates.T,
        long_skip.reshape(1, features),
    )
    batch = math.gcd(tiles, 4)
    columns = pl.BlockSpec((rows, batch * LANES), lambda i: (0, i))
    return pl.pallas_call(
        functools.partial(finish, poles, width),
        grid=(tiles // batch,),
        out_shape=jax.ShapeDtypeStruct(stripe, BF16),
        in_specs=[
            columns,
            columns,
            pl.BlockSpec((batch, SUB, 2 * heads * poles), lambda i: (i, 0, 0)),
            pl.BlockSpec((batch, poles, blocks * LANES), lambda i: (i, 0, 0)),
        ],
        out_specs=columns,
        compiler_params=pltpu.CompilerParams(vmem_limit_bytes=16 * 1024 * 1024),
    )(gate_out, part, dw, before)


def solution(mesh):
    rows = P(("grp", "seq"), None)
    in_specs = (rows, rows, rows, rows, P(), P(), P(), P(), P())
    return jax.shard_map(shards, mesh=mesh, in_specs=in_specs, out_specs=rows, check_vma=False)
```

```python
import functools

import jax
import jax.numpy as jnp
from jax import lax
from jax.experimental import pallas as pl
from jax.experimental.pallas import tpu as pltpu
from jax.sharding import PartitionSpec as P

SUB = 128
LANES = 128
STRIP = 64
MESH = pl.DeviceIdType.MESH
F32 = jnp.float32
BF16 = jnp.bfloat16


def iota(shape, axis):
    return lax.broadcasted_iota(jnp.int32, shape, axis)


def dot(a, b):
    return jnp.dot(a, b, preferred_element_type=F32)


def toeplitz(row, shift):
    return pltpu.roll(jnp.broadcast_to(row, (STRIP, SUB)), shift, 1, stride=1, stride_axis=0)


def choose(parts, index):
    bit = 1
    while len(parts) > 1:
        odd = lax.rem(index // bit, 2) == 1
        parts = [jnp.where(odd, parts[k + 1], parts[k]) for k in range(0, len(parts), 2)]
        bit *= 2
    return parts[0]


def thirds(x):
    high = x.astype(BF16)
    rest = x - high.astype(F32)
    middle = rest.astype(BF16)
    return [high, middle, (rest - middle.astype(F32)).astype(BF16)]


def kernel(
    n,
    owners,
    blocks,
    width,
    poles,
    q_hbm,
    a_hbm,
    v_hbm,
    k_hbm,
    taps_ref,
    mskip_ref,
    res_ref,
    rates_ref,
    lskip_ref,
    out_hbm,
    q_ref,
    a_ref,
    v_ref,
    k_ref,
    ext_ref,
    part_ref,
    o_ref,
    lhsm_refs,
    lhsl_refs,
    line_ref,
    fold_ref,
    dw_ref,
    r0_ref,
    rp_ref,
    sp_ref,
    s0_ref,
    st_ref,
    gath_ref,
    cret_ref,
    cin_ref,
    in_sem,
    out_sem,
    halo_send,
    halo_recv,
    st_send,
    st_recv,
    c_send,
    c_recv,
):
    rows, features = q_hbm.shape
    tiles = features // LANES
    per_owner = tiles // owners
    chunk = per_owner * LANES
    heads = LANES // width
    half = heads // 2
    wide = blocks * LANES
    tail = rows - SUB
    me = lax.axis_index("seq")

    barrier = pltpu.get_barrier_semaphore()

    def greet(i, _):
        @pl.when(i != me)
        def _():
            pl.semaphore_signal(barrier, inc=1, device_id={"seq": i}, device_id_type=MESH)

        return 0

    lax.fori_loop(0, n, greet, 0)

    loads = [
        pltpu.make_async_copy(a_hbm.at[pl.ds(tail, SUB)], a_ref.at[pl.ds(tail, SUB)], in_sem.at[0]),
        pltpu.make_async_copy(v_hbm.at[pl.ds(tail, SUB)], v_ref.at[pl.ds(tail, SUB)], in_sem.at[1]),
        pltpu.make_async_copy(a_hbm.at[pl.ds(0, tail)], a_ref.at[pl.ds(0, tail)], in_sem.at[2]),
        pltpu.make_async_copy(v_hbm.at[pl.ds(0, tail)], v_ref.at[pl.ds(0, tail)], in_sem.at[3]),
        pltpu.make_async_copy(k_hbm, k_ref, in_sem.at[4]),
        pltpu.make_async_copy(q_hbm, q_ref, in_sem.at[5]),
    ]
    for load in loads:
        load.start()

    def lanes_of(t):
        return pl.ds(pl.multiple_of(t * LANES, LANES), LANES)

    def chunk_of(o):
        return pl.ds(pl.multiple_of(o * chunk, chunk), chunk)

    def multiply(start, count, cols):
        ext_ref[pl.ds(SUB + start, count), cols] = (
            a_ref[pl.ds(start, count), cols].astype(F32) * v_ref[pl.ds(start, count), cols].astype(F32)
        ).astype(BF16)

    def halo(o):
        return pltpu.make_async_remote_copy(
            src_ref=ext_ref.at[pl.ds(rows, SUB), chunk_of(o)],
            dst_ref=ext_ref.at[pl.ds(0, SUB), chunk_of(o)],
            send_sem=halo_send.at[o],
            recv_sem=halo_recv.at[o],
            device_id={"seq": jnp.minimum(me + 1, n - 1)},
            device_id_type=MESH,
        )

    loads[0].wait()
    loads[1].wait()
    pl.semaphore_wait(barrier, n - 1)

    def send_halo(i, _):
        o = lax.rem(me + 1 + i, owners)
        multiply(tail, SUB, chunk_of(o))

        @pl.when(me < n - 1)
        def _():
            halo(o).start()

        return 0

    lax.fori_loop(0, owners, send_halo, 0)

    @pl.when(me == 0)
    def _():
        ext_ref[pl.ds(0, SUB), :] = jnp.zeros((SUB, features), BF16)

    loads[2].wait()
    loads[3].wait()

    def rest(o, _):
        multiply(0, tail, chunk_of(o))
        return 0

    lax.fori_loop(0, owners, rest, 0)

    row_id = iota((SUB, SUB), 0)
    col_id = iota((SUB, SUB), 1)
    strip_row, strip_col = iota((STRIP, SUB), 0), iota((STRIP, SUB), 1)
    below = strip_col <= strip_row
    inside = strip_col <= strip_row + (SUB - STRIP)
    zero = jnp.zeros((STRIP, SUB), F32)
    mirror = (lax.rem(row_id + col_id, SUB) == 0).astype(BF16)
    r0_ref[...] = dot(taps_ref[...], mirror)
    table = jnp.concatenate(thirds(rates_ref[...]) + thirds(res_ref[...]), axis=0)
    groups = rates_ref.shape[1]
    pick_row, pick_col = iota((groups, LANES), 0), iota((groups, LANES), 1) // width

    def column(x):
        return jnp.concatenate(
            [jnp.broadcast_to(x[:, g * width : g * width + 1], (poles, LANES)) for g in range(heads)], axis=0
        )

    def tables(t):
        spread = dot(table, (pick_row == t * heads + pick_col).astype(F32).astype(BF16))
        spread = [spread[m * poles : (m + 1) * poles] for m in range(6)]
        rp = spread[0] + spread[1] + spread[2]
        sp = spread[3] + spread[4] + spread[5]
        rp_ref[t] = rp
        sp_ref[t] = sp
        rate_col, res_col = column(rp), column(sp)
        fold = jnp.exp(-rate_col * (SUB - 1 - col_id).astype(F32))
        weighted = (res_col * fold).reshape(heads, poles, SUB).sum(axis=1)
        line_ref[t] = pltpu.roll(weighted, 1, 1).astype(BF16).astype(F32)
        middle = half * poles
        fold_ref[t] = jnp.concatenate([fold[:middle], fold[middle:]], axis=1).astype(BF16)

    def tables_of(o, _):
        for k in range(per_owner):
            tables(o * per_owner + k)
        return 0

    lax.fori_loop(0, owners, tables_of, 0)

    def weights(t, k, slot):
        lhsm_ref, lhsl_ref = lhsm_refs[slot], lhsl_refs[slot]
        line = line_ref[t]
        lhsl_ref[k, pl.ds(half * STRIP, half * poles), :] = fold_ref[t]
        for r in range(half):
            first = jnp.where(inside, toeplitz(line[r : r + 1], SUB - STRIP), zero)
            second = jnp.where(inside, toeplitz(line[r + half : r + half + 1], SUB - STRIP), zero)
            lhsl_ref[k, pl.ds(r * STRIP, STRIP), :] = jnp.concatenate([first, second], axis=1).astype(BF16)
        for g in range(heads):
            band = toeplitz(r0_ref[pl.ds(t * heads + g, 1), :], 0)
            lhsm_ref[k, pl.ds(g * STRIP, STRIP), :] = jnp.concatenate(
                [jnp.where(below, zero, band), jnp.where(below, band, zero)], axis=1
            ).astype(BF16)

    def reach_of(t):
        rate_col, res_col = column(rp_ref[t]), column(sp_ref[t])
        reach = (res_col * jnp.exp(-rate_col * (col_id + 1).astype(F32))).T
        high = reach.astype(BF16)
        dw_ref[t] = jnp.concatenate([high, (reach - high.astype(F32)).astype(BF16)], axis=1)

    def reaches(o, _):
        for k in range(per_owner):
            reach_of(o * per_owner + k)
        return 0

    for k in range(per_owner):
        weights(lax.rem(me, owners) * per_owner + k, k, 0)
    loads[4].wait()

    lane_head = iota((8, LANES), 1) // width
    lane_head = jnp.concatenate([lane_head] * blocks, axis=1)
    strip_head = jnp.concatenate([lane_head] * (STRIP // 8), axis=0)
    state_head = jnp.concatenate([lane_head] * (poles // 8), axis=0)
    low = jnp.concatenate([lane_head] * (SUB // 8), axis=0) < half

    def state_out(o):
        return pltpu.make_async_remote_copy(
            src_ref=st_ref.at[pl.ds(o * per_owner, per_owner)],
            dst_ref=gath_ref.at[me],
            send_sem=st_send.at[o],
            recv_sem=st_recv.at[me],
            device_id={"seq": o},
            device_id_type=MESH,
        )

    def side(ref, cols):
        return jnp.concatenate([ref[pl.ds(b * SUB, SUB), cols].astype(F32) for b in range(blocks)], axis=1)

    def main(t, k, slot):
        lhsm_ref, lhsl_ref = lhsm_refs[slot], lhsl_refs[slot]
        cols = lanes_of(t)
        reach = SUB + STRIP
        medium = []
        for start in range(0, SUB, STRIP):
            rhs = jnp.concatenate([ext_ref[pl.ds(b * SUB + start, reach), cols] for b in range(blocks)], axis=1)
            many = dot(lhsm_ref[k, :, :reach], rhs)
            medium.append(choose([many[g * STRIP : (g + 1) * STRIP] for g in range(heads)], strip_head))
        medium = jnp.concatenate(medium, axis=0)
        product = jnp.concatenate([ext_ref[pl.ds((b + 1) * SUB, SUB), cols] for b in range(blocks)], axis=1)
        skip = jnp.concatenate([mskip_ref[:, cols]] * blocks, axis=1)
        medium = medium + skip * product.astype(F32)
        gated = (side(k_ref, cols) * medium).astype(BF16).astype(F32)
        pad = jnp.zeros((SUB - STRIP, wide), BF16)
        first = jnp.concatenate([pad, jnp.where(low, gated, 0.0).astype(BF16)], axis=0)
        second = jnp.concatenate([pad, jnp.where(low, 0.0, gated).astype(BF16)], axis=0)
        inner = []
        for start in range(0, SUB, STRIP):
            pair = jnp.concatenate([first[start : start + SUB], second[start : start + SUB]], axis=0)
            last = start + STRIP == SUB
            many = dot(lhsl_ref[k] if last else lhsl_ref[k, : half * STRIP], pair)
            inner.append(choose([many[r * STRIP : (r + 1) * STRIP] for r in range(half)], strip_head))
        inner = jnp.concatenate(inner, axis=0)
        base = half * STRIP
        states = choose([many[base + r * poles : base + (r + 1) * poles] for r in range(half)], state_head)
        inner = inner + jnp.concatenate([lskip_ref[:, cols]] * blocks, axis=1) * gated
        decay = jnp.exp(rp_ref[t] * (-1.0 * SUB))
        held = jnp.zeros((poles, LANES), F32)
        for b in range(blocks):
            part_ref[pl.ds(b * SUB, SUB), cols] = inner[:, b * LANES : (b + 1) * LANES]
            s0_ref[t, b] = held
            held = decay * held + states[:, b * LANES : (b + 1) * LANES]
        st_ref[t] = held.astype(BF16)

    def step(i, slot):
        o = lax.rem(me + i, owners)
        later = lax.rem(me + i + 1, owners)

        @pl.when(me > 0)
        def _():
            halo(o).wait_recv()

        for k in range(per_owner):
            main(o * per_owner + k, k, slot)
            weights(later * per_owner + k, k, 1 - slot)

        @pl.when(o != me)
        def _():
            state_out(o).start()

    def work(j, _):
        step(2 * j, 0)
        step(2 * j + 1, 1)
        return 0

    lax.fori_loop(0, owners // 2, work, 0)
    lax.fori_loop(0, owners // 2, reaches, 0)

    def carry_back(e):
        return pltpu.make_async_remote_copy(
            src_ref=cret_ref.at[e],
            dst_ref=cin_ref.at[pl.ds(me * per_owner, per_owner)],
            send_sem=c_send.at[e],
            recv_sem=c_recv.at[me],
            device_id={"seq": e},
            device_id_type=MESH,
        )

    def state_in(e):
        return pltpu.make_async_remote_copy(
            src_ref=st_ref.at[pl.ds(0, per_owner)],
            dst_ref=gath_ref.at[e],
            send_sem=st_send.at[0],
            recv_sem=st_recv.at[e],
            device_id={"seq": e},
            device_id_type=MESH,
        )

    def carry_in(o):
        return pltpu.make_async_remote_copy(
            src_ref=cret_ref.at[0],
            dst_ref=cin_ref.at[pl.ds(o * per_owner, per_owner)],
            send_sem=c_send.at[0],
            recv_sem=c_recv.at[o],
            device_id={"seq": o},
            device_id_type=MESH,
        )

    @pl.when(me < owners)
    def _():
        mine = pl.ds(me * per_owner, per_owner)
        gath_ref[me] = st_ref[mine]
        power = jnp.exp(rp_ref[mine] * (-1.0 * SUB * blocks))

        def scan(e, held):
            cret_ref[e] = held.astype(BF16)

            @pl.when(e != me)
            def _():
                state_in(e).wait_recv()

            return power * held + gath_ref[e].astype(F32)

        lax.fori_loop(0, n, scan, jnp.zeros((per_owner, poles, LANES), F32))

        def give(i, _):
            carry_back(lax.rem(me + i, n)).start()
            return 0

        lax.fori_loop(1, n, give, 0)
        cin_ref[mine] = cret_ref[me]

    lax.fori_loop(owners // 2, owners, reaches, 0)
    loads[5].wait()

    def result(o):
        return pltpu.make_async_copy(o_ref.at[:, chunk_of(o)], out_hbm.at[:, chunk_of(o)], out_sem.at[o])

    spot = iota((heads * poles, wide), 0) // poles == lax.rem(iota((heads * poles, wide), 1), LANES) // width

    def finish(t):
        cols = lanes_of(t)
        decay = jnp.exp(rp_ref[t] * (-1.0 * SUB))
        carried = cin_ref[t].astype(F32)
        before = []
        for b in range(blocks):
            before.append(carried + s0_ref[t, b])
            carried = decay * carried
        before = jnp.concatenate(before, axis=1)
        spread = jnp.where(spot, jnp.concatenate([before] * heads, axis=0), 0.0)
        high = spread.astype(BF16)
        low = (spread - high.astype(F32)).astype(BF16)
        reach = dot(dw_ref[t], jnp.concatenate([high, high], axis=0)) + dot(dw_ref[t, :, : heads * poles], low)
        for b in range(blocks):
            at = pl.ds(b * SUB, SUB)
            o_ref[at, cols] = (
                q_ref[at, cols].astype(F32) * (part_ref[at, cols] + reach[:, b * LANES : (b + 1) * LANES])
            ).astype(BF16)

    def closing(i, _):
        o = lax.rem(me + owners - i, owners) if n == owners else i

        @pl.when(o != me)
        def _():
            carry_in(o).wait_recv()

        for k in range(per_owner):
            finish(o * per_owner + k)
        result(o).start()
        return 0

    lax.fori_loop(0, owners, closing, 0)

    def drain(o, _):
        result(o).wait()

        @pl.when(o != me)
        def _():
            state_out(o).wait_send()

        @pl.when(me < n - 1)
        def _():
            halo(o).wait_send()

        return 0

    lax.fori_loop(0, owners, drain, 0)

    @pl.when(me < owners)
    def _():
        def drain_carry(e, _):
            @pl.when(e != me)
            def _():
                carry_back(e).wait_send()

            return 0

        lax.fori_loop(0, n, drain_carry, 0)


def hand_on(from_ref, to_ref, sem):
    count = sem.shape[0]
    share = from_ref.shape[0] // count
    copies = [
        pltpu.make_async_copy(from_ref.at[pl.ds(k * share, share)], to_ref.at[pl.ds(k * share, share)], sem.at[k])
        for k in range(count)
    ]
    for copy in copies:
        copy.start()
    for copy in copies:
        copy.wait()


def shards(
    gate_out, gate_in, values, gate_mid, medium_taps, medium_skip, residues, rates, long_skip
):
    rows, features = gate_out.shape
    groups, poles = rates.shape
    width = features // groups
    blocks = rows // SUB
    tiles = features // LANES
    n = lax.axis_size("seq")
    owners = min(n, tiles)
    per_owner = tiles // owners
    heads = LANES // width
    stripe = (rows, features)
    vmem = pl.BlockSpec(memory_space=pltpu.VMEM)
    hbm = pl.BlockSpec(memory_space=pl.ANY)
    flops = 2 * tiles * SUB * 2 * SUB * blocks * LANES * (heads + heads // 2 + 2)
    mixed = pl.pallas_call(
        functools.partial(kernel, n, owners, blocks, width, poles),
        out_shape=jax.ShapeDtypeStruct(stripe, BF16),
        in_specs=[hbm] * 4 + [vmem] * 5,
        out_specs=hbm,
        scratch_shapes=[
            pltpu.VMEM(stripe, BF16),
            pltpu.VMEM(stripe, BF16),
            pltpu.VMEM(stripe, BF16),
            pltpu.VMEM(stripe, BF16),
            pltpu.VMEM((rows + SUB, features), BF16),
            pltpu.VMEM(stripe, F32),
            pltpu.VMEM(stripe, BF16),
            [pltpu.VMEM((per_owner, heads * STRIP, 2 * SUB), BF16)] * 2,
            [pltpu.VMEM((per_owner, heads // 2 * (STRIP + poles), 2 * SUB), BF16)] * 2,
            pltpu.VMEM((tiles, heads, SUB), F32),
            pltpu.VMEM((tiles, heads // 2 * poles, 2 * SUB), BF16),
            pltpu.VMEM((tiles, SUB, 2 * heads * poles), BF16),
            pltpu.VMEM((groups, SUB), F32),
            pltpu.VMEM((tiles, poles, LANES), F32),
            pltpu.VMEM((tiles, poles, LANES), F32),
            pltpu.VMEM((tiles, blocks, poles, LANES), F32),
            pltpu.VMEM((tiles, poles, LANES), BF16),
            pltpu.VMEM((n, per_owner, poles, LANES), BF16),
            pltpu.VMEM((n, per_owner, poles, LANES), BF16),
            pltpu.VMEM((tiles, poles, LANES), BF16),
            pltpu.SemaphoreType.DMA((6,)),
            pltpu.SemaphoreType.DMA((owners,)),
            pltpu.SemaphoreType.DMA((owners,)),
            pltpu.SemaphoreType.DMA((owners,)),
            pltpu.SemaphoreType.DMA((owners,)),
            pltpu.SemaphoreType.DMA((n,)),
            pltpu.SemaphoreType.DMA((n,)),
            pltpu.SemaphoreType.DMA((owners,)),
        ],
        compiler_params=pltpu.CompilerParams(
            collective_id=0, has_side_effects=True, vmem_limit_bytes=60 * 1024 * 1024
        ),
        cost_estimate=pl.CostEstimate(flops=flops, bytes_accessed=10 * rows * features, transcendentals=0),
    )(
        gate_out,
        gate_in,
        values,
        gate_mid,
        medium_taps,
        medium_skip.reshape(1, features),
        residues.T,
        rates.T,
        long_skip.reshape(1, features),
    )
    return pl.pallas_call(
        hand_on,
        out_shape=jax.ShapeDtypeStruct(stripe, BF16),
        in_specs=[hbm],
        out_specs=hbm,
        scratch_shapes=[pltpu.SemaphoreType.DMA((rows // 16,))],
        compiler_params=pltpu.CompilerParams(vmem_limit_bytes=60 * 1024 * 1024),
    )(mixed)


def solution(mesh):
    rows = P(("grp", "seq"), None)
    in_specs = (rows, rows, rows, rows, P(), P(), P(), P(), P())
    return jax.shard_map(shards, mesh=mesh, in_specs=in_specs, out_specs=rows, check_vma=False)
```

```python
import functools

import jax
import jax.numpy as jnp
from jax import lax
from jax.experimental import pallas as pl
from jax.experimental.pallas import tpu as pltpu
from jax.sharding import PartitionSpec as P

SUB = 128
LANES = 128
STRIP = 32
MESH = pl.DeviceIdType.MESH
F32 = jnp.float32
BF16 = jnp.bfloat16


def iota(shape, axis):
    return lax.broadcasted_iota(jnp.int32, shape, axis)


def dot(a, b):
    return jnp.dot(a, b, preferred_element_type=F32)


def toeplitz(row, shift):
    return pltpu.roll(jnp.broadcast_to(row, (STRIP, SUB)), shift, 1, stride=1, stride_axis=0)


def thirds(x):
    high = x.astype(BF16)
    rest = x - high.astype(F32)
    middle = rest.astype(BF16)
    return [high, middle, (rest - middle.astype(F32)).astype(BF16)]


def kernel(
    n,
    owners,
    blocks,
    width,
    poles,
    q_hbm,
    a_hbm,
    v_hbm,
    k_hbm,
    taps_ref,
    mskip_ref,
    res_ref,
    rates_ref,
    lskip_ref,
    out_hbm,
    q_ref,
    a_ref,
    v_ref,
    k_ref,
    ext_ref,
    part_ref,
    o_ref,
    lhsm_refs,
    lhsl_refs,
    rpm_refs,
    dw_ref,
    r0_ref,
    rp_ref,
    sp_ref,
    s0_ref,
    st_ref,
    gath_ref,
    cret_ref,
    cin_ref,
    in_sem,
    out_sem,
    halo_send,
    halo_recv,
    st_send,
    st_recv,
    c_send,
    c_recv,
):
    rows, features = q_hbm.shape
    tiles = features // LANES
    per_owner = tiles // owners
    chunk = per_owner * LANES
    heads = LANES // width
    half = heads // 2
    wide = blocks * LANES
    tail = rows - SUB
    me = lax.axis_index("seq")

    barrier = pltpu.get_barrier_semaphore()

    def greet(i, _):
        @pl.when(i != me)
        def _():
            pl.semaphore_signal(barrier, inc=1, device_id={"seq": i}, device_id_type=MESH)

        return 0

    lax.fori_loop(0, n, greet, 0)

    loads = [
        pltpu.make_async_copy(a_hbm.at[pl.ds(tail, SUB)], a_ref.at[pl.ds(tail, SUB)], in_sem.at[0]),
        pltpu.make_async_copy(v_hbm.at[pl.ds(tail, SUB)], v_ref.at[pl.ds(tail, SUB)], in_sem.at[1]),
        pltpu.make_async_copy(a_hbm.at[pl.ds(0, tail)], a_ref.at[pl.ds(0, tail)], in_sem.at[2]),
        pltpu.make_async_copy(v_hbm.at[pl.ds(0, tail)], v_ref.at[pl.ds(0, tail)], in_sem.at[3]),
        pltpu.make_async_copy(k_hbm, k_ref, in_sem.at[4]),
        pltpu.make_async_copy(q_hbm, q_ref, in_sem.at[5]),
    ]
    for load in loads:
        load.start()

    def lanes_of(t):
        return pl.ds(pl.multiple_of(t * LANES, LANES), LANES)

    def chunk_of(o):
        return pl.ds(pl.multiple_of(o * chunk, chunk), chunk)

    def multiply(start, count, cols):
        ext_ref[pl.ds(SUB + start, count), cols] = (
            a_ref[pl.ds(start, count), cols].astype(F32) * v_ref[pl.ds(start, count), cols].astype(F32)
        ).astype(BF16)

    def halo(o):
        return pltpu.make_async_remote_copy(
            src_ref=ext_ref.at[pl.ds(rows, SUB), chunk_of(o)],
            dst_ref=ext_ref.at[pl.ds(0, SUB), chunk_of(o)],
            send_sem=halo_send.at[o],
            recv_sem=halo_recv.at[o],
            device_id={"seq": jnp.minimum(me + 1, n - 1)},
            device_id_type=MESH,
        )

    loads[0].wait()
    loads[1].wait()
    pl.semaphore_wait(barrier, n - 1)

    def send_halo(i, _):
        o = lax.rem(me + 1 + i, owners)
        multiply(tail, SUB, chunk_of(o))

        @pl.when(me < n - 1)
        def _():
            halo(o).start()

        return 0

    lax.fori_loop(0, owners, send_halo, 0)

    @pl.when(me == 0)
    def _():
        ext_ref[pl.ds(0, SUB), :] = jnp.zeros((SUB, features), BF16)

    loads[2].wait()
    loads[3].wait()

    def rest(o, _):
        multiply(0, tail, chunk_of(o))
        return 0

    lax.fori_loop(0, owners, rest, 0)

    row_id = iota((SUB, SUB), 0)
    col_id = iota((SUB, SUB), 1)
    strip_row, strip_col = iota((STRIP, SUB), 0), iota((STRIP, SUB), 1)
    below = strip_col <= strip_row
    inside = strip_col <= strip_row + (SUB - STRIP)
    zero = jnp.zeros((STRIP, SUB), F32)
    mirror = (lax.rem(row_id + col_id, SUB) == 0).astype(BF16)
    r0_ref[...] = dot(taps_ref[...], mirror)
    table = jnp.concatenate(thirds(rates_ref[...]) + thirds(res_ref[...]), axis=0)
    groups = rates_ref.shape[1]
    pick_row, pick_col = iota((groups, LANES), 0), iota((groups, LANES), 1) // width

    def column(x):
        return jnp.concatenate(
            [jnp.broadcast_to(x[:, g * width : g * width + 1], (poles, LANES)) for g in range(heads)], axis=0
        )

    def weights(t, k, slot):
        lhsm_ref, lhsl_ref = lhsm_refs[slot], lhsl_refs[slot]
        spread = dot(table, (pick_row == t * heads + pick_col).astype(F32).astype(BF16))
        spread = [spread[m * poles : (m + 1) * poles] for m in range(6)]
        rp = spread[0] + spread[1] + spread[2]
        sp = spread[3] + spread[4] + spread[5]
        rp_ref[t] = rp
        sp_ref[t] = sp
        rpm_refs[slot][k] = rp
        rate_col, res_col = column(rp), column(sp)
        fold = jnp.exp(-rate_col * (SUB - 1 - col_id).astype(F32))
        weighted = (res_col * fold).reshape(heads, poles, SUB).sum(axis=1)
        line = pltpu.roll(weighted, 1, 1).astype(BF16).astype(F32)
        for r in range(half):
            first = jnp.where(inside, toeplitz(line[r : r + 1], SUB - STRIP), zero)
            second = jnp.where(inside, toeplitz(line[r + half : r + half + 1], SUB - STRIP), zero)
            lhsl_ref[k, pl.ds(r * STRIP, STRIP), :] = jnp.concatenate([first, second], axis=1).astype(BF16)
            lhsl_ref[k, pl.ds(half * STRIP + r * poles, poles), :] = jnp.concatenate(
                [fold[r * poles : (r + 1) * poles], fold[(r + half) * poles : (r + half + 1) * poles]], axis=1
            ).astype(BF16)
        for g in range(heads):
            band = toeplitz(r0_ref[pl.ds(t * heads + g, 1), :], 0)
            lhsm_ref[k, pl.ds(g * STRIP, STRIP), :] = jnp.concatenate(
                [jnp.where(below, zero, band), jnp.where(below, band, zero)], axis=1
            ).astype(BF16)

    def reach_of(t):
        rate_col, res_col = column(rp_ref[t]), column(sp_ref[t])
        reach = (res_col * jnp.exp(-rate_col * (col_id + 1).astype(F32))).T
        high = reach.astype(BF16)
        dw_ref[t] = jnp.concatenate([high, (reach - high.astype(F32)).astype(BF16)], axis=1)

    def reaches(o, _):
        for k in range(per_owner):
            reach_of(o * per_owner + k)
        return 0

    for k in range(per_owner):
        weights(lax.rem(me, owners) * per_owner + k, k, 0)
    loads[4].wait()

    strip_head = lax.rem(iota((STRIP, wide), 1), LANES) // width
    state_head = lax.rem(iota((poles, wide), 1), LANES) // width
    low = lax.rem(iota((SUB, wide), 1), LANES) // width < half

    def state_out(o):
        return pltpu.make_async_remote_copy(
            src_ref=st_ref.at[pl.ds(o * per_owner, per_owner)],
            dst_ref=gath_ref.at[me],
            send_sem=st_send.at[o],
            recv_sem=st_recv.at[me],
            device_id={"seq": o},
            device_id_type=MESH,
        )

    def side(ref, cols):
        return jnp.concatenate([ref[pl.ds(b * SUB, SUB), cols].astype(F32) for b in range(blocks)], axis=1)

    def main(t, k, slot):
        lhsm_ref, lhsl_ref = lhsm_refs[slot], lhsl_refs[slot]
        cols = lanes_of(t)
        reach = SUB + STRIP
        medium = []
        for start in range(0, SUB, STRIP):
            rhs = jnp.concatenate([ext_ref[pl.ds(b * SUB + start, reach), cols] for b in range(blocks)], axis=1)
            many = dot(lhsm_ref[k, :, :reach], rhs)
            strip = many[:STRIP]
            for g in range(1, heads):
                strip = jnp.where(strip_head == g, many[g * STRIP : (g + 1) * STRIP], strip)
            medium.append(strip)
        medium = jnp.concatenate(medium, axis=0)
        product = jnp.concatenate([ext_ref[pl.ds((b + 1) * SUB, SUB), cols] for b in range(blocks)], axis=1)
        skip = jnp.concatenate([mskip_ref[:, cols]] * blocks, axis=1)
        medium = medium + skip * product.astype(F32)
        gated = (side(k_ref, cols) * medium).astype(BF16).astype(F32)
        pad = jnp.zeros((SUB - STRIP, wide), BF16)
        first = jnp.concatenate([pad, jnp.where(low, gated, 0.0).astype(BF16)], axis=0)
        second = jnp.concatenate([pad, jnp.where(low, 0.0, gated).astype(BF16)], axis=0)
        inner = []
        for start in range(0, SUB, STRIP):
            pair = jnp.concatenate([first[start : start + SUB], second[start : start + SUB]], axis=0)
            last = start + STRIP == SUB
            many = dot(lhsl_ref[k] if last else lhsl_ref[k, : half * STRIP], pair)
            strip = many[:STRIP]
            for r in range(1, half):
                strip = jnp.where(lax.rem(strip_head, half) == r, many[r * STRIP : (r + 1) * STRIP], strip)
            inner.append(strip)
        inner = jnp.concatenate(inner, axis=0)
        base = half * STRIP
        states = many[base : base + poles]
        for r in range(1, half):
            states = jnp.where(
                lax.rem(state_head, half) == r, many[base + r * poles : base + (r + 1) * poles], states
            )
        inner = inner + jnp.concatenate([lskip_ref[:, cols]] * blocks, axis=1) * gated
        decay = jnp.exp(rpm_refs[slot][k] * (-1.0 * SUB))
        held = jnp.zeros((poles, LANES), F32)
        for b in range(blocks):
            part_ref[pl.ds(b * SUB, SUB), cols] = inner[:, b * LANES : (b + 1) * LANES]
            s0_ref[t, b] = held
            held = decay * held + states[:, b * LANES : (b + 1) * LANES]
        st_ref[t] = held.astype(BF16)

    def step(i, slot):
        o = lax.rem(me + i, owners)
        later = lax.rem(me + i + 1, owners)

        @pl.when(me > 0)
        def _():
            halo(o).wait_recv()

        for k in range(per_owner):
            main(o * per_owner + k, k, slot)
            weights(later * per_owner + k, k, 1 - slot)

        @pl.when(o != me)
        def _():
            state_out(o).start()

    def work(j, _):
        step(2 * j, 0)
        step(2 * j + 1, 1)
        return 0

    lax.fori_loop(0, owners // 2, work, 0)
    lax.fori_loop(0, owners // 2, reaches, 0)

    def carry_back(e):
        return pltpu.make_async_remote_copy(
            src_ref=cret_ref.at[e],
            dst_ref=cin_ref.at[pl.ds(me * per_owner, per_owner)],
            send_sem=c_send.at[e],
            recv_sem=c_recv.at[me],
            device_id={"seq": e},
            device_id_type=MESH,
        )

    def state_in(e):
        return pltpu.make_async_remote_copy(
            src_ref=st_ref.at[pl.ds(0, per_owner)],
            dst_ref=gath_ref.at[e],
            send_sem=st_send.at[0],
            recv_sem=st_recv.at[e],
            device_id={"seq": e},
            device_id_type=MESH,
        )

    def carry_in(o):
        return pltpu.make_async_remote_copy(
            src_ref=cret_ref.at[0],
            dst_ref=cin_ref.at[pl.ds(o * per_owner, per_owner)],
            send_sem=c_send.at[0],
            recv_sem=c_recv.at[o],
            device_id={"seq": o},
            device_id_type=MESH,
        )

    @pl.when(me < owners)
    def _():
        mine = pl.ds(me * per_owner, per_owner)
        gath_ref[me] = st_ref[mine]
        power = jnp.exp(rp_ref[mine] * (-1.0 * SUB * blocks))

        def scan(e, held):
            cret_ref[e] = held.astype(BF16)

            @pl.when(e != me)
            def _():
                state_in(e).wait_recv()

            return power * held + gath_ref[e].astype(F32)

        lax.fori_loop(0, n, scan, jnp.zeros((per_owner, poles, LANES), F32))

        def give(i, _):
            carry_back(lax.rem(me + i, n)).start()
            return 0

        lax.fori_loop(1, n, give, 0)
        cin_ref[mine] = cret_ref[me]

    lax.fori_loop(owners // 2, owners, reaches, 0)
    loads[5].wait()

    def result(o):
        return pltpu.make_async_copy(o_ref.at[:, chunk_of(o)], out_hbm.at[:, chunk_of(o)], out_sem.at[o])

    spot = iota((heads * poles, wide), 0) // poles == lax.rem(iota((heads * poles, wide), 1), LANES) // width

    def finish(t):
        cols = lanes_of(t)
        decay = jnp.exp(rp_ref[t] * (-1.0 * SUB))
        carried = cin_ref[t].astype(F32)
        before = []
        for b in range(blocks):
            before.append(carried + s0_ref[t, b])
            carried = decay * carried
        before = jnp.concatenate(before, axis=1)
        spread = jnp.where(spot, jnp.concatenate([before] * heads, axis=0), 0.0)
        high = spread.astype(BF16)
        low = (spread - high.astype(F32)).astype(BF16)
        reach = dot(dw_ref[t], jnp.concatenate([high, high], axis=0)) + dot(dw_ref[t, :, : heads * poles], low)
        for b in range(blocks):
            at = pl.ds(b * SUB, SUB)
            o_ref[at, cols] = (
                q_ref[at, cols].astype(F32) * (part_ref[at, cols] + reach[:, b * LANES : (b + 1) * LANES])
            ).astype(BF16)

    def closing(i, _):
        o = lax.rem(me + owners - i, owners) if n == owners else i

        @pl.when(o != me)
        def _():
            carry_in(o).wait_recv()

        for k in range(per_owner):
            finish(o * per_owner + k)
        result(o).start()
        return 0

    lax.fori_loop(0, owners, closing, 0)

    def drain(o, _):
        result(o).wait()

        @pl.when(o != me)
        def _():
            state_out(o).wait_send()

        @pl.when(me < n - 1)
        def _():
            halo(o).wait_send()

        return 0

    lax.fori_loop(0, owners, drain, 0)

    @pl.when(me < owners)
    def _():
        def drain_carry(e, _):
            @pl.when(e != me)
            def _():
                carry_back(e).wait_send()

            return 0

        lax.fori_loop(0, n, drain_carry, 0)


def hand_on(from_ref, to_ref):
    to_ref[...] = from_ref[...]


def shards(
    gate_out, gate_in, values, gate_mid, medium_taps, medium_skip, residues, rates, long_skip
):
    rows, features = gate_out.shape
    groups, poles = rates.shape
    width = features // groups
    blocks = rows // SUB
    tiles = features // LANES
    n = lax.axis_size("seq")
    owners = min(n, tiles)
    per_owner = tiles // owners
    heads = LANES // width
    stripe = (rows, features)
    vmem = pl.BlockSpec(memory_space=pltpu.VMEM)
    hbm = pl.BlockSpec(memory_space=pl.ANY)
    flops = 2 * tiles * SUB * 2 * SUB * blocks * LANES * (heads + heads // 2 + 2)
    mixed = pl.pallas_call(
        functools.partial(kernel, n, owners, blocks, width, poles),
        out_shape=jax.ShapeDtypeStruct(stripe, BF16),
        in_specs=[hbm] * 4 + [vmem] * 5,
        out_specs=hbm,
        scratch_shapes=[
            pltpu.VMEM(stripe, BF16),
            pltpu.VMEM(stripe, BF16),
            pltpu.VMEM(stripe, BF16),
            pltpu.VMEM(stripe, BF16),
            pltpu.VMEM((rows + SUB, features), BF16),
            pltpu.VMEM(stripe, F32),
            pltpu.VMEM(stripe, BF16),
            [pltpu.VMEM((per_owner, heads * STRIP, 2 * SUB), BF16)] * 2,
            [pltpu.VMEM((per_owner, heads // 2 * (STRIP + poles), 2 * SUB), BF16)] * 2,
            [pltpu.VMEM((per_owner, poles, LANES), F32)] * 2,
            pltpu.VMEM((tiles, SUB, 2 * heads * poles), BF16),
            pltpu.VMEM((groups, SUB), F32),
            pltpu.VMEM((tiles, poles, LANES), F32),
            pltpu.VMEM((tiles, poles, LANES), F32),
            pltpu.VMEM((tiles, blocks, poles, LANES), F32),
            pltpu.VMEM((tiles, poles, LANES), BF16),
            pltpu.VMEM((n, per_owner, poles, LANES), BF16),
            pltpu.VMEM((n, per_owner, poles, LANES), BF16),
            pltpu.VMEM((tiles, poles, LANES), BF16),
            pltpu.SemaphoreType.DMA((6,)),
            pltpu.SemaphoreType.DMA((owners,)),
            pltpu.SemaphoreType.DMA((owners,)),
            pltpu.SemaphoreType.DMA((owners,)),
            pltpu.SemaphoreType.DMA((owners,)),
            pltpu.SemaphoreType.DMA((n,)),
            pltpu.SemaphoreType.DMA((n,)),
            pltpu.SemaphoreType.DMA((owners,)),
        ],
        compiler_params=pltpu.CompilerParams(
            collective_id=0, has_side_effects=True, vmem_limit_bytes=60 * 1024 * 1024
        ),
        cost_estimate=pl.CostEstimate(flops=flops, bytes_accessed=10 * rows * features, transcendentals=0),
    )(
        gate_out,
        gate_in,
        values,
        gate_mid,
        medium_taps,
        medium_skip.reshape(1, features),
        residues.T,
        rates.T,
        long_skip.reshape(1, features),
    )
    band = pl.BlockSpec((rows // 4, features), lambda i: (i, 0))
    return pl.pallas_call(
        hand_on,
        grid=(4,),
        out_shape=jax.ShapeDtypeStruct(stripe, BF16),
        in_specs=[band],
        out_specs=band,
        compiler_params=pltpu.CompilerParams(vmem_limit_bytes=60 * 1024 * 1024),
    )(mixed)


def solution(mesh):
    rows = P(("grp", "seq"), None)
    in_specs = (rows, rows, rows, rows, P(), P(), P(), P(), P())
    return jax.shard_map(shards, mesh=mesh, in_specs=in_specs, out_specs=rows, check_vma=False)
```
